32 devices in a mesh: row: 8 (over y, x, core), col: 4 (over z).
Axes of the slice: x: 2, y: 2, z: 4, core: 2. Of those that a mesh axis runs over, the one named last changes fastest.
Arguments:
- x_tiles: bfloat16 [128, 8, 256, 256], P(('row', 'col')), as said below
- columns: int32 [128, 8], P(('row', 'col')), may hold values from 0 to 127, as said below
- branch: int32 [8, 2], P('row'), may hold values from 0 to 1
Outputs:
- purified: float32 [128, 8, 256, 256], P(('row', 'col'))
- occupation: float32 [8], P('row')
The draws below stay inside these ranges and needn't reach their ends.
Inputs may be any that keep to these rules, and one draw needn't show every extreme that they name: `columns`: block rows form fragments of 16 consecutive rows, each with two halves of 8 rows. Slot 0 of a block row is the row itself; its other slots hold, in ascending order, every row of the other half of its fragment but one, so that the pattern is symmetric and no two rows of one half are coupled. `x_tiles`: every tile of the pattern is the transpose of its mirror tile, and diagonal tiles are symmetric.
All inputs are finite; a program needn't handle non-finite values.
Results may differ from the reference program's by a relative error of at most 0.0028.
Values may be sent and summed in bfloat16 or wider, within the bound.
A program may use at most 128 MiB of HBM per device.

```python
import jax
import jax.numpy as jnp
from jax import lax

TS = 256
TPR = 8
CLUSTER = 16
STEPS = 2
NB = 128
FRAGMENTS = 8


def pattern_parts(key):
    clusters = NB // CLUSTER
    half_rows = CLUSTER // 2
    cluster_keys = jax.random.split(jax.random.fold_in(key, 11), clusters)
    orderings = jax.vmap(lambda subkey: jax.random.permutation(subkey, half_rows))(cluster_keys).astype(jnp.int32)
    inverse = jnp.argsort(orderings, axis=1).astype(jnp.int32)
    offsets = jnp.arange(half_rows - 1, dtype=jnp.int32)
    upper_rows = half_rows + offsets[None, None, :] + (offsets[None, None, :] >= orderings[:, :, None]).astype(jnp.int32)
    lower_rows = offsets[None, None, :] + (offsets[None, None, :] >= inverse[:, :, None]).astype(jnp.int32)
    partners = jnp.concatenate([upper_rows, lower_rows], axis=1)
    itself = jnp.broadcast_to(jnp.arange(CLUSTER, dtype=jnp.int32)[None, :, None], (clusters, CLUSTER, 1))
    local_cols = jnp.concatenate([itself, partners], axis=2)
    row_base = (jnp.arange(clusters, dtype=jnp.int32) * CLUSTER)[:, None, None]
    return ((local_cols + row_base).reshape(NB, TPR), lower_rows, orderings)


def draw_columns(key, part):
    return pattern_parts(key)[0]


def draw_x_tiles(key, part):
    clusters = NB // CLUSTER
    half_rows = CLUSTER // 2
    unused, lower_rows, orderings = pattern_parts(key)
    sample_key = jax.random.fold_in(key, 3)
    samples = jax.random.normal(sample_key, (clusters, CLUSTER, TPR, TS, TS), jnp.float32)
    spread = 0.9 / (TS * TPR) ** 0.5
    diagonal = (samples[:, :, 0] + jnp.swapaxes(samples[:, :, 0], 2, 3)) * (spread / 2.0 ** 0.5)
    first_half = samples[:, :half_rows]
    upper_tiles = first_half[:, :, 1:] * spread
    row_ids = jnp.arange(half_rows, dtype=jnp.int32)[None, :, None]
    order_at = jax.vmap(lambda order, index_set: order[index_set])(orderings, lower_rows)
    slot_ids = 1 + row_ids - (row_ids > order_at).astype(jnp.int32)
    picked = jax.vmap(lambda block, index_set, slot_set: block[index_set, slot_set])(first_half, lower_rows, slot_ids)
    lower_tiles = jnp.swapaxes(picked, 3, 4) * spread
    upper_block = jnp.concatenate([diagonal[:, :half_rows, None], upper_tiles], axis=2)
    lower_block = jnp.concatenate([diagonal[:, half_rows:, None], lower_tiles], axis=2)
    return jnp.concatenate([upper_block, lower_block], axis=1).reshape(NB, TPR, TS, TS).astype(jnp.bfloat16)


def touch_ends(array, own_key, least, top_value):
    dims = array.shape
    index_at = [jax.random.randint(jax.random.fold_in(own_key, axis), (), 0, dims[axis]) for axis in range(len(dims))]
    array = array.at[tuple(index_at)].set(least)
    longest = dims.index(max(dims))
    index_at[longest] = (index_at[longest] + 1) % dims[longest]
    return array.at[tuple(index_at)].set(top_value)


def setup_inputs(seed: int = 0) -> dict:
    arg_keys = jax.random.split(jax.random.key(seed), 4)
    x_tiles = draw_x_tiles(jax.random.fold_in(arg_keys[3], 71), 0)
    columns = draw_columns(jax.random.fold_in(arg_keys[3], 71), 0)
    branch = touch_ends(jax.random.randint(arg_keys[2], (FRAGMENTS, STEPS), 0, 2), jax.random.fold_in(arg_keys[2], 1), 0, 1).astype(jnp.int32)
    return {"x_tiles": x_tiles, "columns": columns, "branch": branch}


def advance(tiles_in, cols_in, step_sign):
    tile_size = tiles_in.shape[-1]
    row_count = tiles_in.shape[0]
    rounded = tiles_in.astype(jnp.bfloat16).astype(jnp.float32)
    diagonal = rounded[:, 0]
    diagonal_sum = jnp.einsum("ctij,ctkj->cik", rounded, rounded, precision=lax.Precision.HIGHEST)
    local_term = jnp.einsum("cij,csjk->csik", diagonal, rounded[:, 1:], precision=lax.Precision.HIGHEST)
    partner = cols_in[:, 1:]
    matches = cols_in[partner] == jnp.arange(row_count, dtype=jnp.int32)[:, None, None]
    back_slot = jnp.argmax(matches, axis=2).astype(jnp.int32) - 1
    mirrored = local_term[partner, back_slot]
    partner_term = lax.optimization_barrier(jnp.swapaxes(mirrored, 2, 3).astype(jnp.bfloat16)).astype(jnp.float32)
    identity = jnp.eye(tile_size, dtype=jnp.float32)
    new_diagonal = tiles_in[:, 0] + step_sign * (diagonal_sum - 0.25 * identity)
    new_others = tiles_in[:, 1:] + step_sign * (local_term + partner_term)
    return jnp.concatenate([new_diagonal[:, None], new_others], axis=1)


def reference(x_tiles, columns, branch):
    clusters = NB // CLUSTER
    tiles = x_tiles.astype(jnp.float32).reshape(clusters, CLUSTER, TPR, TS, TS)
    local_cols = (columns % CLUSTER).astype(jnp.int32).reshape(clusters, CLUSTER, TPR)
    signs = (2 * branch - 1).astype(jnp.float32)

    def purify(inputs):
        current, cols_in, sign_row = inputs
        for iteration in range(STEPS):
            current = advance(current, cols_in, sign_row[iteration])
        trace_sum = jnp.sum(jnp.diagonal(current[:, 0], axis1=1, axis2=2))
        return current, trace_sum / (CLUSTER * TS) + 0.5

    purified, occupation = lax.map(purify, (tiles, local_cols, signs))
    return purified.reshape(NB, TPR, TS, TS), occupation
```

```python
import functools

import jax
import jax.numpy as jnp
from jax import lax
from jax.experimental import pallas as pl
from jax.experimental.pallas import tpu as pltpu
from jax.sharding import PartitionSpec as P

MESH = pl.DeviceIdType.MESH
HEAD = 16
NN = (((1,), (0,)), ((), ()))
NT = (((1,), (1,)), ((), ()))


def mm(a, b, dims=NN):
    return lax.dot_general(a, b, dims, preferred_element_type=jnp.float32)


def purify_kernel(
    n, cols_ref, branch_ref, x_hbm, out_ref, occ_ref,
    x, d1, send, recv, gath, trace, load_sem, send_sem, recv_sem, pass_sem, tsend_sem, trecv_sem,
):
    rows, slots, size = x.shape[0], x.shape[1], x.shape[2]
    half_tile = size // 2
    h = n // 2
    half_rows = rows * h
    me = lax.axis_index("col")
    upper = (me >= h).astype(jnp.int32)
    mine = me - upper * h
    dist = jnp.where(me < h, h - 1 - me, me - h)
    target = jnp.where(me < h, h, h - 1)
    onward = jnp.where(me < h, me - 1, me + 1)

    load_diag = pltpu.make_async_copy(x_hbm.at[:, 0:1], x.at[:, 0:1], load_sem.at[0])
    load_rest = pltpu.make_async_copy(x_hbm.at[:, 1:slots], x.at[:, 1:slots], load_sem.at[1])
    load_diag.start()
    load_rest.start()

    barrier = pltpu.get_barrier_semaphore()
    for k in range(1, n):
        pl.semaphore_signal(barrier, inc=1, device_id={"col": lax.rem(me + k, n)}, device_id_type=MESH)

    signs = [(2 * branch_ref[0, step] - 1).astype(jnp.float32) for step in range(2)]
    ri = lax.broadcasted_iota(jnp.int32, (half_tile, half_tile), 0)
    ci = lax.broadcasted_iota(jnp.int32, (half_tile, half_tile), 1)
    head_row = lax.broadcasted_iota(jnp.int32, (HEAD, half_tile), 0)
    eye = (
        lax.broadcasted_iota(jnp.int32, (size, size), 0) == lax.broadcasted_iota(jnp.int32, (size, size), 1)
    )

    def chunk(t):
        return (0, HEAD + size) if t == 0 else (HEAD + t * size, size)

    def pack(tile, step, t, head):
        a11 = tile[:half_tile, :half_tile]
        a22 = tile[half_tile:, half_tile:]
        at = pl.multiple_of(HEAD + t * size, HEAD)
        send[step, pl.ds(at, half_tile), :] = jnp.where(ri <= ci, a11, a22).astype(jnp.bfloat16)
        send[step, pl.ds(at + half_tile, half_tile), :] = tile[:half_tile, half_tile:].astype(jnp.bfloat16)
        corner = jnp.sum(jnp.where(ri == ci, a22, 0.0), axis=0, keepdims=True)
        return head + jnp.where(head_row == t, corner, 0.0)

    def own_copy(step, t):
        at, length = chunk(t)
        return pltpu.make_async_remote_copy(
            src_ref=send.at[step, pl.ds(at, length)],
            dst_ref=recv.at[step, mine, pl.ds(at, length)],
            send_sem=send_sem.at[step, t],
            recv_sem=recv_sem.at[step, mine, t],
            device_id={"col": target},
            device_id_type=MESH,
        )

    def pass_copy(step, r, t):
        at, length = chunk(t)
        return pltpu.make_async_remote_copy(
            src_ref=recv.at[step, r, pl.ds(at, length)],
            dst_ref=recv.at[step, r, pl.ds(at, length)],
            send_sem=pass_sem.at[step, r, t],
            recv_sem=recv_sem.at[step, r, t],
            device_id={"col": onward},
            device_id_type=MESH,
        )

    def arrive(step, t):
        for r in range(h):
            pass_copy(step, r, t).wait_recv()

            @pl.when(dist < h - 1)
            def _():
                pass_copy(step, r, t).start()

    def unpack(step, t):
        for r in range(h):
            at = HEAD + t * size
            mixed = recv[step, r, pl.ds(at, half_tile), :].astype(jnp.float32)
            cross = recv[step, r, pl.ds(at + half_tile, half_tile), :]
            head = recv[step, r, 0:HEAD, :].astype(jnp.float32)
            corner = jnp.sum(jnp.where(head_row == t, head, 0.0), axis=0, keepdims=True)
            turned = mixed.T
            a11 = jnp.where(ri <= ci, mixed, turned)
            a22 = jnp.where(ri > ci, mixed, jnp.where(ri == ci, corner, turned))
            g = r * rows + t
            gath[step, g, 0:half_tile, 0:half_tile] = a11.astype(jnp.bfloat16)
            gath[step, g, half_tile:, half_tile:] = a22.astype(jnp.bfloat16)
            gath[step, g, 0:half_tile, half_tile:] = cross
            gath[step, g, half_tile:, 0:half_tile] = cross.astype(jnp.float32).T.astype(jnp.bfloat16)

    def ready(t):
        return [
            s for s in range(slots - 1)
            if max(s % rows, (s + 1) % rows) == t
        ]

    def other(step, i, s):
        first = lax.rem(cols_ref[i, s + 1], half_rows) == s
        return lax.select(first, gath[step, s], gath[step, s + 1])

    load_diag.wait()
    head = jnp.zeros((HEAD, half_tile), jnp.float32)
    for t in range(rows):
        head = pack(x[t, 0].astype(jnp.float32), 0, t, head)
    send[0, 0:HEAD, :] = head.astype(jnp.bfloat16)
    pl.semaphore_wait(barrier, n - 1)
    for t in range(rows):
        own_copy(0, t).start()

    load_rest.wait()

    def first_diagonal(i, head):
        total = mm(x[i, 0], x[i, 0], NT)
        for s in range(1, slots):
            total += mm(x[i, s], x[i, s], NT)
        new = x[i, 0].astype(jnp.float32) + signs[0] * (total - jnp.where(eye, 0.25, 0.0))
        out_ref[i, 0] = new
        d1[i, 0] = new.astype(jnp.bfloat16)
        return pack(new, 1, i, head)

    head = lax.fori_loop(0, rows, first_diagonal, jnp.zeros((HEAD, half_tile), jnp.float32))
    send[1, 0:HEAD, :] = head.astype(jnp.bfloat16)
    for t in range(rows):
        own_copy(1, t).start()

    def first_local(i, carry):
        for s in range(1, slots):
            out_ref[i, s] = x[i, s].astype(jnp.float32) + signs[0] * mm(x[i, 0], x[i, s])
        return carry

    lax.fori_loop(0, rows, first_local, 0)

    for t in range(rows):
        arrive(0, t)
        unpack(0, t)
        todo = ready(t)

        def first_partner(i, carry):
            for s in todo:
                new = out_ref[i, s + 1] + signs[0] * mm(x[i, s + 1], other(0, i, s))
                low = new.astype(jnp.bfloat16)
                d1[i, s + 1] = low
                out_ref[i, s + 1] = new + signs[1] * mm(d1[i, 0], low)
            return carry

        if todo:
            lax.fori_loop(0, rows, first_partner, 0)

    arrive(1, 0)
    unpack(1, 0)

    def second_diagonal(i, carry):
        total = mm(d1[i, 0], d1[i, 0], NT)
        for s in range(1, slots):
            total += mm(d1[i, s], d1[i, s], NT)
        new = out_ref[i, 0] + signs[1] * (total - jnp.where(eye, 0.25, 0.0))
        out_ref[i, 0] = new
        on_diag = jnp.where(eye, new, 0.0)
        return carry + jnp.sum(jnp.sum(on_diag.reshape(size // 8, 8, 2, half_tile), axis=0), axis=1)

    lanes = lax.fori_loop(0, rows, second_diagonal, jnp.zeros((8, half_tile), jnp.float32))
    trace[me] = lanes

    def trace_copy(k):
        return pltpu.make_async_remote_copy(
            src_ref=trace.at[me],
            dst_ref=trace.at[me],
            send_sem=tsend_sem.at[k],
            recv_sem=trecv_sem.at[k],
            device_id={"col": lax.rem(me + k, n)},
            device_id_type=MESH,
        )

    def trace_landing(k):
        source = lax.rem(me + n - k, n)
        return pltpu.make_async_remote_copy(
            src_ref=trace.at[source],
            dst_ref=trace.at[source],
            send_sem=tsend_sem.at[k],
            recv_sem=trecv_sem.at[k],
            device_id={"col": lax.rem(me + k, n)},
            device_id_type=MESH,
        )

    for k in range(1, n):
        trace_copy(k).start()

    for t in range(rows):
        if t > 0:
            arrive(1, t)
            unpack(1, t)
        todo = ready(t)

        def second_partner(i, carry):
            for s in todo:
                out_ref[i, s + 1] = out_ref[i, s + 1] + signs[1] * mm(d1[i, s + 1], other(1, i, s))
            return carry

        if todo:
            lax.fori_loop(0, rows, second_partner, 0)

    for k in range(1, n):
        trace_landing(k).wait_recv()
        trace_copy(k).wait_send()
    total = trace[0]
    for k in range(1, n):
        total = total + trace[k]
    scale = 1.0 / (rows * n * size)
    occ_ref[...] = jnp.broadcast_to(jnp.sum(total, keepdims=True) * scale + 0.5, occ_ref.shape)

    for step in range(2):
        for t in range(rows):
            own_copy(step, t).wait_send()

    @pl.when(dist < h - 1)
    def _():
        for step in range(2):
            for r in range(h):
                for t in range(rows):
                    pass_copy(step, r, t).wait_send()


def write_kernel(held, out_hbm, sem):
    copies = [
        pltpu.make_async_copy(held.at[i], out_hbm.at[i], sem.at[i]) for i in range(held.shape[0])
    ]
    for copy in copies:
        copy.start()
    for copy in copies:
        copy.wait()


def shards(n, x_tiles, columns, branch):
    rows, slots, size = x_tiles.shape[0], x_tiles.shape[1], x_tiles.shape[2]
    h = n // 2
    length = HEAD + rows * size
    vmem = pl.BlockSpec(memory_space=pltpu.VMEM)
    smem = pl.BlockSpec(memory_space=pltpu.SMEM)
    flops = 2 * size**3 * rows * (slots * 2 + (slots - 1) * 4)
    held, occ = pl.pallas_call(
        functools.partial(purify_kernel, n),
        out_shape=(
            pltpu.VMEM(x_tiles.shape, jnp.float32),
            jax.ShapeDtypeStruct((8, 128), jnp.float32),
        ),
        in_specs=[smem, smem, pl.BlockSpec(memory_space=pltpu.HBM)],
        out_specs=(vmem, vmem),
        scratch_shapes=[
            pltpu.VMEM((rows, slots, size, size), jnp.bfloat16),
            pltpu.VMEM((rows, slots, size, size), jnp.bfloat16),
            pltpu.VMEM((2, length, size // 2), jnp.bfloat16),
            pltpu.VMEM((2, h, length, size // 2), jnp.bfloat16),
            pltpu.VMEM((2, h * rows, size, size), jnp.bfloat16),
            pltpu.VMEM((n, 8, size // 2), jnp.float32),
            pltpu.SemaphoreType.DMA((2,)),
            pltpu.SemaphoreType.DMA((2, rows)),
            pltpu.SemaphoreType.DMA((2, h, rows)),
            pltpu.SemaphoreType.DMA((2, h, rows)),
            pltpu.SemaphoreType.DMA((n,)),
            pltpu.SemaphoreType.DMA((n,)),
        ],
        compiler_params=pltpu.CompilerParams(
            collective_id=0, has_side_effects=True, vmem_limit_bytes=40 * 2**20
        ),
        cost_estimate=pl.CostEstimate(flops=flops, bytes_accessed=3 * x_tiles.size * 2, transcendentals=0),
        name="purify",
    )(columns, branch, x_tiles)
    purified = pl.pallas_call(
        write_kernel,
        out_shape=jax.ShapeDtypeStruct(x_tiles.shape, jnp.float32),
        in_specs=[vmem],
        out_specs=pl.BlockSpec(memory_space=pl.ANY),
        scratch_shapes=[pltpu.SemaphoreType.DMA((rows,))],
        cost_estimate=pl.CostEstimate(flops=0, bytes_accessed=x_tiles.size * 4, transcendentals=0),
        name="write",
    )(held)
    return purified, occ[0, 0:1]


def solution(mesh):
    placed = (P(("row", "col"), None, None, None), P(("row", "col"), None), P("row", None))
    return jax.shard_map(
        functools.partial(shards, mesh.shape["col"]),
        mesh=mesh,
        in_specs=placed,
        out_specs=(P(("row", "col"), None, None, None), P("row")),
        check_vma=False,
    )
```

```python
import functools

import jax
import jax.numpy as jnp
from jax import lax
from jax.experimental import pallas as pl
from jax.experimental.pallas import tpu as pltpu
from jax.sharding import PartitionSpec as P

MESH = pl.DeviceIdType.MESH
HEAD = 16
NN = (((1,), (0,)), ((), ()))
NT = (((1,), (1,)), ((), ()))


def mm(a, b, dims=NN):
    return lax.dot_general(a, b, dims, preferred_element_type=jnp.float32)


def purify_kernel(
    n, cols_hbm, branch_hbm, x_hbm, out_ref, occ_ref,
    cols_ref, branch_ref, x, d1, send, recv, gath, trace, load_sem, send_sem, recv_sem, pass_sem, tsend_sem, trecv_sem,
):
    rows, slots, size = x.shape[0], x.shape[1], x.shape[2]
    half_tile = size // 2
    h = n // 2
    half_rows = rows * h
    me = lax.axis_index("col")
    upper = (me >= h).astype(jnp.int32)
    mine = me - upper * h
    dist = jnp.where(me < h, h - 1 - me, me - h)
    target = jnp.where(me < h, h, h - 1)
    onward = jnp.where(me < h, me - 1, me + 1)

    load_diag = pltpu.make_async_copy(x_hbm.at[:, 0:1], x.at[:, 0:1], load_sem.at[0])
    load_rest = pltpu.make_async_copy(x_hbm.at[:, 1:slots], x.at[:, 1:slots], load_sem.at[1])
    load_diag.start()
    load_cols = pltpu.make_async_copy(cols_hbm, cols_ref, load_sem.at[2])
    load_branch = pltpu.make_async_copy(branch_hbm, branch_ref, load_sem.at[3])
    load_cols.start()
    load_branch.start()
    load_rest.start()

    barrier = pltpu.get_barrier_semaphore()
    for k in range(1, n):
        pl.semaphore_signal(barrier, inc=1, device_id={"col": lax.rem(me + k, n)}, device_id_type=MESH)

    load_cols.wait()
    load_branch.wait()
    signs = [(2 * branch_ref[0, step] - 1).astype(jnp.float32) for step in range(2)]
    ri = lax.broadcasted_iota(jnp.int32, (half_tile, half_tile), 0)
    ci = lax.broadcasted_iota(jnp.int32, (half_tile, half_tile), 1)
    head_row = lax.broadcasted_iota(jnp.int32, (HEAD, half_tile), 0)
    eye = (
        lax.broadcasted_iota(jnp.int32, (size, size), 0) == lax.broadcasted_iota(jnp.int32, (size, size), 1)
    )

    def chunk(t):
        return (0, HEAD + size) if t == 0 else (HEAD + t * size, size)

    def pack(tile, step, t, head):
        a11 = tile[:half_tile, :half_tile]
        a22 = tile[half_tile:, half_tile:]
        at = pl.multiple_of(HEAD + t * size, HEAD)
        send[step, pl.ds(at, half_tile), :] = jnp.where(ri <= ci, a11, a22).astype(jnp.bfloat16)
        send[step, pl.ds(at + half_tile, half_tile), :] = tile[:half_tile, half_tile:].astype(jnp.bfloat16)
        corner = jnp.sum(jnp.where(ri == ci, a22, 0.0), axis=0, keepdims=True)
        return head + jnp.where(head_row == t, corner, 0.0)

    def own_copy(step, t):
        at, length = chunk(t)
        return pltpu.make_async_remote_copy(
            src_ref=send.at[step, pl.ds(at, length)],
            dst_ref=recv.at[step, mine, pl.ds(at, length)],
            send_sem=send_sem.at[step, t],
            recv_sem=recv_sem.at[step, mine, t],
            device_id={"col": target},
            device_id_type=MESH,
        )

    def pass_copy(step, r, t):
        at, length = chunk(t)
        return pltpu.make_async_remote_copy(
            src_ref=recv.at[step, r, pl.ds(at, length)],
            dst_ref=recv.at[step, r, pl.ds(at, length)],
            send_sem=pass_sem.at[step, r, t],
            recv_sem=recv_sem.at[step, r, t],
            device_id={"col": onward},
            device_id_type=MESH,
        )

    def arrive(step, t):
        for r in range(h):
            pass_copy(step, r, t).wait_recv()

            @pl.when(dist < h - 1)
            def _():
                pass_copy(step, r, t).start()

    def unpack(step, t):
        for r in range(h):
            at = HEAD + t * size
            mixed = recv[step, r, pl.ds(at, half_tile), :].astype(jnp.float32)
            cross = recv[step, r, pl.ds(at + half_tile, half_tile), :]
            head = recv[step, r, 0:HEAD, :].astype(jnp.float32)
            corner = jnp.sum(jnp.where(head_row == t, head, 0.0), axis=0, keepdims=True)
            turned = mixed.T
            a11 = jnp.where(ri <= ci, mixed, turned)
            a22 = jnp.where(ri > ci, mixed, jnp.where(ri == ci, corner, turned))
            g = r * rows + t
            gath[step, g, 0:half_tile, 0:half_tile] = a11.astype(jnp.bfloat16)
            gath[step, g, half_tile:, half_tile:] = a22.astype(jnp.bfloat16)
            gath[step, g, 0:half_tile, half_tile:] = cross
            gath[step, g, half_tile:, 0:half_tile] = cross.astype(jnp.float32).T.astype(jnp.bfloat16)

    def ready(t):
        return [
            s for s in range(slots - 1)
            if max(s % rows, (s + 1) % rows) == t
        ]

    def other(step, i, s):
        first = lax.rem(cols_ref[i, s + 1], half_rows) == s
        return lax.select(first, gath[step, s], gath[step, s + 1])

    load_diag.wait()
    head = jnp.zeros((HEAD, half_tile), jnp.float32)
    for t in range(rows):
        head = pack(x[t, 0].astype(jnp.float32), 0, t, head)
    send[0, 0:HEAD, :] = head.astype(jnp.bfloat16)
    pl.semaphore_wait(barrier, n - 1)
    for t in range(rows):
        own_copy(0, t).start()

    load_rest.wait()

    def first_diagonal(i, head):
        total = mm(x[i, 0], x[i, 0], NT)
        for s in range(1, slots):
            total += mm(x[i, s], x[i, s], NT)
        new = x[i, 0].astype(jnp.float32) + signs[0] * (total - jnp.where(eye, 0.25, 0.0))
        out_ref[i, 0] = new
        d1[i, 0] = new.astype(jnp.bfloat16)
        return pack(new, 1, i, head)

    head = lax.fori_loop(0, rows, first_diagonal, jnp.zeros((HEAD, half_tile), jnp.float32))
    send[1, 0:HEAD, :] = head.astype(jnp.bfloat16)
    for t in range(rows):
        own_copy(1, t).start()

    def first_local(i, carry):
        for s in range(1, slots):
            out_ref[i, s] = x[i, s].astype(jnp.float32) + signs[0] * mm(x[i, 0], x[i, s])
        return carry

    lax.fori_loop(0, rows, first_local, 0, unroll=True)

    for t in range(rows):
        arrive(0, t)
        unpack(0, t)
        todo = ready(t)

        def first_partner(i, carry):
            for s in todo:
                new = out_ref[i, s + 1] + signs[0] * mm(x[i, s + 1], other(0, i, s))
                low = new.astype(jnp.bfloat16)
                d1[i, s + 1] = low
                out_ref[i, s + 1] = new + signs[1] * mm(d1[i, 0], low)
            return carry

        if todo:
            lax.fori_loop(0, rows, first_partner, 0, unroll=True)

    arrive(1, 0)
    unpack(1, 0)

    def second_diagonal(i, carry):
        total = mm(d1[i, 0], d1[i, 0], NT)
        for s in range(1, slots):
            total += mm(d1[i, s], d1[i, s], NT)
        new = out_ref[i, 0] + signs[1] * (total - jnp.where(eye, 0.25, 0.0))
        out_ref[i, 0] = new
        on_diag = jnp.where(eye, new, 0.0)
        return carry + jnp.sum(jnp.sum(on_diag.reshape(size // 8, 8, 2, half_tile), axis=0), axis=1)

    lanes = lax.fori_loop(0, rows, second_diagonal, jnp.zeros((8, half_tile), jnp.float32))
    trace[me] = lanes

    def trace_copy(k):
        return pltpu.make_async_remote_copy(
            src_ref=trace.at[me],
            dst_ref=trace.at[me],
            send_sem=tsend_sem.at[k],
            recv_sem=trecv_sem.at[k],
            device_id={"col": lax.rem(me + k, n)},
            device_id_type=MESH,
        )

    def trace_landing(k):
        source = lax.rem(me + n - k, n)
        return pltpu.make_async_remote_copy(
            src_ref=trace.at[source],
            dst_ref=trace.at[source],
            send_sem=tsend_sem.at[k],
            recv_sem=trecv_sem.at[k],
            device_id={"col": lax.rem(me + k, n)},
            device_id_type=MESH,
        )

    for k in range(1, n):
        trace_copy(k).start()

    for t in range(rows):
        if t > 0:
            arrive(1, t)
            unpack(1, t)
        todo = ready(t)

        def second_partner(i, carry):
            for s in todo:
                out_ref[i, s + 1] = out_ref[i, s + 1] + signs[1] * mm(d1[i, s + 1], other(1, i, s))
            return carry

        if todo:
            lax.fori_loop(0, rows, second_partner, 0, unroll=True)

    for k in range(1, n):
        trace_landing(k).wait_recv()
        trace_copy(k).wait_send()
    total = trace[0]
    for k in range(1, n):
        total = total + trace[k]
    scale = 1.0 / (rows * n * size)
    occ_ref[...] = jnp.broadcast_to(jnp.sum(total, keepdims=True) * scale + 0.5, occ_ref.shape)

    for step in range(2):
        for t in range(rows):
            own_copy(step, t).wait_send()

    @pl.when(dist < h - 1)
    def _():
        for step in range(2):
            for r in range(h):
                for t in range(rows):
                    pass_copy(step, r, t).wait_send()


def write_kernel(held, occ_ref, out_hbm, occ_out, sem):
    rows = held.shape[0]
    for i in range(rows):
        pltpu.make_async_copy(held.at[i], out_hbm.at[i], sem.at[i]).start()
    occ_out[...] = occ_ref[0, 0:1]
    for i in range(rows):
        pltpu.make_async_copy(held.at[i], out_hbm.at[i], sem.at[i]).wait()


def shards(n, x_tiles, columns, branch):
    rows, slots, size = x_tiles.shape[0], x_tiles.shape[1], x_tiles.shape[2]
    h = n // 2
    length = HEAD + rows * size
    vmem = pl.BlockSpec(memory_space=pltpu.VMEM)
    hbm = pl.BlockSpec(memory_space=pltpu.HBM)
    flops = 2 * size**3 * rows * (slots * 2 + (slots - 1) * 4)
    held, occ = pl.pallas_call(
        functools.partial(purify_kernel, n),
        out_shape=(
            pltpu.VMEM(x_tiles.shape, jnp.float32),
            pltpu.VMEM((8, 128), jnp.float32),
        ),
        in_specs=[hbm, hbm, hbm],
        out_specs=(vmem, vmem),
        scratch_shapes=[
            pltpu.SMEM(columns.shape, jnp.int32),
            pltpu.SMEM(branch.shape, jnp.int32),
            pltpu.VMEM((rows, slots, size, size), jnp.bfloat16),
            pltpu.VMEM((rows, slots, size, size), jnp.bfloat16),
            pltpu.VMEM((2, length, size // 2), jnp.bfloat16),
            pltpu.VMEM((2, h, length, size // 2), jnp.bfloat16),
            pltpu.VMEM((2, h * rows, size, size), jnp.bfloat16),
            pltpu.VMEM((n, 8, size // 2), jnp.float32),
            pltpu.SemaphoreType.DMA((4,)),
            pltpu.SemaphoreType.DMA((2, rows)),
            pltpu.SemaphoreType.DMA((2, h, rows)),
            pltpu.SemaphoreType.DMA((2, h, rows)),
            pltpu.SemaphoreType.DMA((n,)),
            pltpu.SemaphoreType.DMA((n,)),
        ],
        compiler_params=pltpu.CompilerParams(
            collective_id=0, has_side_effects=True, vmem_limit_bytes=40 * 2**20
        ),
        cost_estimate=pl.CostEstimate(flops=flops, bytes_accessed=3 * x_tiles.size * 2, transcendentals=0),
        name="purify",
    )(*[pltpu.with_memory_space_constraint(a, pltpu.HBM) for a in (columns, branch, x_tiles)])
    return pl.pallas_call(
        write_kernel,
        out_shape=(
            jax.ShapeDtypeStruct(x_tiles.shape, jnp.float32),
            jax.ShapeDtypeStruct((1,), jnp.float32),
        ),
        in_specs=[vmem, vmem],
        out_specs=(hbm, vmem),
        scratch_shapes=[pltpu.SemaphoreType.DMA((rows,))],
        compiler_params=pltpu.CompilerParams(vmem_limit_bytes=4 * 2**20),
        cost_estimate=pl.CostEstimate(flops=0, bytes_accessed=x_tiles.size * 4, transcendentals=0),
        name="write",
    )(
        pltpu.with_memory_space_constraint(held, pltpu.VMEM),
        pltpu.with_memory_space_constraint(occ, pltpu.VMEM),
    )


def solution(mesh):
    placed = (P(("row", "col"), None, None, None), P(("row", "col"), None), P("row", None))
    return jax.shard_map(
        functools.partial(shards, mesh.shape["col"]),
        mesh=mesh,
        in_specs=placed,
        out_specs=(P(("row", "col"), None, None, None), P("row")),
        check_vma=False,
    )
```

```python
import functools

import jax
import jax.numpy as jnp
from jax import lax
from jax.experimental import pallas as pl
from jax.experimental.pallas import tpu as pltpu
from jax.sharding import PartitionSpec as P

MESH = pl.DeviceIdType.MESH
HEAD = 16
WINDOW = 3
NN = (((1,), (0,)), ((), ()))
NT = (((1,), (1,)), ((), ()))


def mm(a, b, dims=NN):
    return lax.dot_general(a, b, dims, preferred_element_type=jnp.float32)


def purify_kernel(
    n, cols_hbm, branch_hbm, x_hbm, out_ref, occ_ref,
    cols_ref, branch_ref, x, d1, send, recv, gath, trace, load_sem, send_sem, recv_sem, pass_sem, tsend_sem, trecv_sem,
):
    rows, slots, size = x.shape[0], x.shape[1], x.shape[2]
    half_tile = size // 2
    h = n // 2
    half_rows = rows * h
    me = lax.axis_index("col")
    upper = (me >= h).astype(jnp.int32)
    mine = me - upper * h
    dist = jnp.where(me < h, h - 1 - me, me - h)
    target = jnp.where(me < h, h, h - 1)
    onward = jnp.where(me < h, me - 1, me + 1)

    load_diag = pltpu.make_async_copy(x_hbm.at[:, 0:1], x.at[:, 0:1], load_sem.at[0])
    load_rest = pltpu.make_async_copy(x_hbm.at[:, 1:slots], x.at[:, 1:slots], load_sem.at[1])
    load_diag.start()
    load_cols = pltpu.make_async_copy(cols_hbm, cols_ref, load_sem.at[2])
    load_branch = pltpu.make_async_copy(branch_hbm, branch_ref, load_sem.at[3])
    load_cols.start()
    load_branch.start()
    load_rest.start()

    barrier = pltpu.get_barrier_semaphore()
    for k in range(1, n):
        pl.semaphore_signal(barrier, inc=1, device_id={"col": lax.rem(me + k, n)}, device_id_type=MESH)

    load_cols.wait()
    load_branch.wait()
    signs = [(2 * branch_ref[0, step] - 1).astype(jnp.float32) for step in range(2)]
    ri = lax.broadcasted_iota(jnp.int32, (half_tile, half_tile), 0)
    ci = lax.broadcasted_iota(jnp.int32, (half_tile, half_tile), 1)
    head_row = lax.broadcasted_iota(jnp.int32, (HEAD, half_tile), 0)
    eye = (
        lax.broadcasted_iota(jnp.int32, (size, size), 0) == lax.broadcasted_iota(jnp.int32, (size, size), 1)
    )

    def piece(k):
        step, q = divmod(k, 2 * rows)
        at, end = HEAD + q * half_tile, HEAD + (q + 1) * half_tile
        at = 0 if q == 0 else at
        return step, q, pl.ds(at, end - at)

    def pack(tile, step, t, head):
        a11 = tile[:half_tile, :half_tile]
        a22 = tile[half_tile:, half_tile:]
        at = pl.multiple_of(HEAD + t * size, HEAD)
        send[step, pl.ds(at, half_tile), :] = jnp.where(ri <= ci, a11, a22).astype(jnp.bfloat16)
        send[step, pl.ds(at + half_tile, half_tile), :] = tile[:half_tile, half_tile:].astype(jnp.bfloat16)
        corner = jnp.sum(jnp.where(ri == ci, a22, 0.0), axis=0, keepdims=True)
        return head + jnp.where(head_row == t, corner, 0.0)

    def own_copy(k):
        step, q, span = piece(k)
        return pltpu.make_async_remote_copy(
            src_ref=send.at[step, span],
            dst_ref=recv.at[step, mine, span],
            send_sem=send_sem.at[step, q],
            recv_sem=recv_sem.at[step, mine, q],
            device_id={"col": target},
            device_id_type=MESH,
        )

    def pass_copy(k, r):
        step, q, span = piece(k)
        return pltpu.make_async_remote_copy(
            src_ref=recv.at[step, r, span],
            dst_ref=recv.at[step, r, span],
            send_sem=pass_sem.at[step, r, q],
            recv_sem=recv_sem.at[step, r, q],
            device_id={"col": onward},
            device_id_type=MESH,
        )

    pieces = 4 * rows
    begun = [0]

    def pump(upto):
        while begun[0] < min(upto, pieces):
            own_copy(begun[0]).start()
            begun[0] += 1

    def arrive(k):
        if begun[0] < pieces:
            own_copy(k).wait_send()
            pump(k + 1 + WINDOW)
        for r in range(h):
            pass_copy(k, r).wait_recv()

            @pl.when(dist < h - 1)
            def _():
                pass_copy(k, r).start()

    def unpack(step, t):
        for r in range(h):
            at = HEAD + t * size
            mixed = recv[step, r, pl.ds(at, half_tile), :].astype(jnp.float32)
            cross = recv[step, r, pl.ds(at + half_tile, half_tile), :]
            head = recv[step, r, 0:HEAD, :].astype(jnp.float32)
            corner = jnp.sum(jnp.where(head_row == t, head, 0.0), axis=0, keepdims=True)
            turned = mixed.T
            a11 = jnp.where(ri <= ci, mixed, turned)
            a22 = jnp.where(ri > ci, mixed, jnp.where(ri == ci, corner, turned))
            g = r * rows + t
            gath[step, g, 0:half_tile, 0:half_tile] = a11.astype(jnp.bfloat16)
            gath[step, g, half_tile:, half_tile:] = a22.astype(jnp.bfloat16)
            gath[step, g, 0:half_tile, half_tile:] = cross
            gath[step, g, half_tile:, 0:half_tile] = cross.astype(jnp.float32).T.astype(jnp.bfloat16)

    def ready(t):
        return [
            s for s in range(slots - 1)
            if max(s % rows, (s + 1) % rows) == t
        ]

    def other(step, i, s):
        first = lax.rem(cols_ref[i, s + 1], half_rows) == s
        return lax.select(first, gath[step, s], gath[step, s + 1])

    load_diag.wait()
    head = jnp.zeros((HEAD, half_tile), jnp.float32)
    for t in range(rows):
        head = pack(x[t, 0].astype(jnp.float32), 0, t, head)
    send[0, 0:HEAD, :] = head.astype(jnp.bfloat16)
    pl.semaphore_wait(barrier, n - 1)
    pump(min(WINDOW, 2 * rows))
    load_rest.wait()

    def first_diagonal(i, head):
        total = mm(x[i, 0], x[i, 0], NT)
        for s in range(1, slots):
            total += mm(x[i, s], x[i, s], NT)
        new = x[i, 0].astype(jnp.float32) + signs[0] * (total - jnp.where(eye, 0.25, 0.0))
        out_ref[i, 0] = new
        d1[i, 0] = new.astype(jnp.bfloat16)
        return pack(new, 1, i, head)

    def first_local(i, carry):
        for s in range(1, slots):
            out_ref[i, s] = x[i, s].astype(jnp.float32) + signs[0] * mm(x[i, 0], x[i, s])
        return carry

    for t in range(rows):
        if t == 0:
            head = lax.fori_loop(0, rows, first_diagonal, jnp.zeros((HEAD, half_tile), jnp.float32))
            send[1, 0:HEAD, :] = head.astype(jnp.bfloat16)
        arrive(2 * t)
        arrive(2 * t + 1)
        if t == 0:
            lax.fori_loop(0, rows, first_local, 0, unroll=True)
        unpack(0, t)
        todo = ready(t)

        def first_partner(i, carry):
            for s in todo:
                new = out_ref[i, s + 1] + signs[0] * mm(x[i, s + 1], other(0, i, s))
                low = new.astype(jnp.bfloat16)
                d1[i, s + 1] = low
                out_ref[i, s + 1] = new + signs[1] * mm(d1[i, 0], low)
            return carry

        if todo:
            lax.fori_loop(0, rows, first_partner, 0, unroll=True)

    arrive(2 * rows)
    arrive(2 * rows + 1)
    unpack(1, 0)

    def second_diagonal(i, carry):
        total = mm(d1[i, 0], d1[i, 0], NT)
        for s in range(1, slots):
            total += mm(d1[i, s], d1[i, s], NT)
        new = out_ref[i, 0] + signs[1] * (total - jnp.where(eye, 0.25, 0.0))
        out_ref[i, 0] = new
        on_diag = jnp.where(eye, new, 0.0)
        return carry + jnp.sum(jnp.sum(on_diag.reshape(size // 8, 8, 2, half_tile), axis=0), axis=1)

    lanes = lax.fori_loop(0, rows, second_diagonal, jnp.zeros((8, half_tile), jnp.float32))
    trace[me] = lanes

    def trace_copy(k):
        return pltpu.make_async_remote_copy(
            src_ref=trace.at[me],
            dst_ref=trace.at[me],
            send_sem=tsend_sem.at[k],
            recv_sem=trecv_sem.at[k],
            device_id={"col": lax.rem(me + k, n)},
            device_id_type=MESH,
        )

    def trace_landing(k):
        source = lax.rem(me + n - k, n)
        return pltpu.make_async_remote_copy(
            src_ref=trace.at[source],
            dst_ref=trace.at[source],
            send_sem=tsend_sem.at[k],
            recv_sem=trecv_sem.at[k],
            device_id={"col": lax.rem(me + k, n)},
            device_id_type=MESH,
        )

    for k in range(1, n):
        trace_copy(k).start()

    for t in range(rows):
        if t > 0:
            arrive(2 * (rows + t))
            arrive(2 * (rows + t) + 1)
            unpack(1, t)
        todo = ready(t)

        def second_partner(i, carry):
            for s in todo:
                out_ref[i, s + 1] = out_ref[i, s + 1] + signs[1] * mm(d1[i, s + 1], other(1, i, s))
            return carry

        if todo:
            lax.fori_loop(0, rows, second_partner, 0, unroll=True)

    for k in range(1, n):
        trace_landing(k).wait_recv()
        trace_copy(k).wait_send()
    total = trace[0]
    for k in range(1, n):
        total = total + trace[k]
    scale = 1.0 / (rows * n * size)
    occ_ref[...] = jnp.broadcast_to(jnp.sum(total, keepdims=True) * scale + 0.5, occ_ref.shape)

    for k in range(max(pieces - WINDOW, 0), pieces):
        own_copy(k).wait_send()

    @pl.when(dist < h - 1)
    def _():
        for k in range(pieces):
            for r in range(h):
                pass_copy(k, r).wait_send()


def write_kernel(held, occ_ref, out_hbm, occ_out, sem):
    rows, slots = held.shape[0], held.shape[1]

    def part(i, j):
        span = pl.ds(2 * j, 2)
        return pltpu.make_async_copy(held.at[i, span], out_hbm.at[i, span], sem.at[i, j])

    for i in range(rows):
        for j in range(slots // 2):
            part(i, j).start()
    occ_out[...] = occ_ref[0, 0:1]
    for i in range(rows):
        for j in range(slots // 2):
            part(i, j).wait()


def shards(n, x_tiles, columns, branch):
    rows, slots, size = x_tiles.shape[0], x_tiles.shape[1], x_tiles.shape[2]
    h = n // 2
    length = HEAD + rows * size
    vmem = pl.BlockSpec(memory_space=pltpu.VMEM)
    hbm = pl.BlockSpec(memory_space=pltpu.HBM)
    flops = 2 * size**3 * rows * (slots * 2 + (slots - 1) * 4)
    held, occ = pl.pallas_call(
        functools.partial(purify_kernel, n),
        out_shape=(
            pltpu.VMEM(x_tiles.shape, jnp.float32),
            pltpu.VMEM((8, 128), jnp.float32),
        ),
        in_specs=[hbm, hbm, hbm],
        out_specs=(vmem, vmem),
        scratch_shapes=[
            pltpu.SMEM(columns.shape, jnp.int32),
            pltpu.SMEM(branch.shape, jnp.int32),
            pltpu.VMEM((rows, slots, size, size), jnp.bfloat16),
            pltpu.VMEM((rows, slots, size, size), jnp.bfloat16),
            pltpu.VMEM((2, length, size // 2), jnp.bfloat16),
            pltpu.VMEM((2, h, length, size // 2), jnp.bfloat16),
            pltpu.VMEM((2, h * rows, size, size), jnp.bfloat16),
            pltpu.VMEM((n, 8, size // 2), jnp.float32),
            pltpu.SemaphoreType.DMA((4,)),
            pltpu.SemaphoreType.DMA((2, 2 * rows)),
            pltpu.SemaphoreType.DMA((2, h, 2 * rows)),
            pltpu.SemaphoreType.DMA((2, h, 2 * rows)),
            pltpu.SemaphoreType.DMA((n,)),
            pltpu.SemaphoreType.DMA((n,)),
        ],
        compiler_params=pltpu.CompilerParams(
            collective_id=0, has_side_effects=True, vmem_limit_bytes=40 * 2**20
        ),
        cost_estimate=pl.CostEstimate(flops=flops, bytes_accessed=3 * x_tiles.size * 2, transcendentals=0),
        name="purify",
    )(*[pltpu.with_memory_space_constraint(a, pltpu.HBM) for a in (columns, branch, x_tiles)])
    return pl.pallas_call(
        write_kernel,
        out_shape=(
            jax.ShapeDtypeStruct(x_tiles.shape, jnp.float32),
            jax.ShapeDtypeStruct((1,), jnp.float32),
        ),
        in_specs=[vmem, vmem],
        out_specs=(hbm, vmem),
        scratch_shapes=[pltpu.SemaphoreType.DMA((rows, slots // 2))],
        compiler_params=pltpu.CompilerParams(vmem_limit_bytes=4 * 2**20),
        cost_estimate=pl.CostEstimate(flops=0, bytes_accessed=x_tiles.size * 4, transcendentals=0),
        name="write",
    )(
        pltpu.with_memory_space_constraint(held, pltpu.VMEM),
        pltpu.with_memory_space_constraint(occ, pltpu.VMEM),
    )


def solution(mesh):
    placed = (P(("row", "col"), None, None, None), P(("row", "col"), None), P("row", None))
    return jax.shard_map(
        functools.partial(shards, mesh.shape["col"]),
        mesh=mesh,
        in_specs=placed,
        out_specs=(P(("row", "col"), None, None, None), P("row")),
        check_vma=False,
    )
```

```python
import functools

import jax
import jax.numpy as jnp
from jax import lax
from jax.experimental import pallas as pl
from jax.experimental.pallas import tpu as pltpu
from jax.sharding import PartitionSpec as P

MESH = pl.DeviceIdType.MESH
HEAD = 16
WINDOW = 4
AHEAD = 2
NN = (((1,), (0,)), ((), ()))
NT = (((1,), (1,)), ((), ()))


def mm(a, b, dims=NN):
    return lax.dot_general(a, b, dims, preferred_element_type=jnp.float32)


def purify_kernel(
    n, cols_hbm, branch_hbm, x_hbm, out_ref, occ_ref,
    cols_ref, branch_ref, x, d1, send, recv, gath, trace, load_sem, send_sem, recv_sem, pass_sem, tsend_sem, trecv_sem,
):
    rows, slots, size = x.shape[0], x.shape[1], x.shape[2]
    half_tile = size // 2
    h = n // 2
    half_rows = rows * h
    me = lax.axis_index("col")
    upper = (me >= h).astype(jnp.int32)
    mine = me - upper * h
    first = upper * h
    mirror = n - 1 - me
    theirs = h - 1 - mine

    load_diag = pltpu.make_async_copy(x_hbm.at[:, 0:1], x.at[:, 0:1], load_sem.at[0])
    load_rest = pltpu.make_async_copy(x_hbm.at[:, 1:slots], x.at[:, 1:slots], load_sem.at[1])
    load_diag.start()
    load_cols = pltpu.make_async_copy(cols_hbm, cols_ref, load_sem.at[2])
    load_branch = pltpu.make_async_copy(branch_hbm, branch_ref, load_sem.at[3])
    load_cols.start()
    load_branch.start()
    load_rest.start()

    barrier = pltpu.get_barrier_semaphore()
    for k in range(1, n):
        pl.semaphore_signal(barrier, inc=1, device_id={"col": lax.rem(me + k, n)}, device_id_type=MESH)

    load_cols.wait()
    load_branch.wait()
    signs = [(2 * branch_ref[0, step] - 1).astype(jnp.float32) for step in range(2)]
    ri = lax.broadcasted_iota(jnp.int32, (half_tile, half_tile), 0)
    ci = lax.broadcasted_iota(jnp.int32, (half_tile, half_tile), 1)
    head_row = lax.broadcasted_iota(jnp.int32, (HEAD, half_tile), 0)
    eye = (
        lax.broadcasted_iota(jnp.int32, (size, size), 0) == lax.broadcasted_iota(jnp.int32, (size, size), 1)
    )

    def piece(k):
        step, q = divmod(k, 2 * rows)
        at, end = HEAD + q * half_tile, HEAD + (q + 1) * half_tile
        at = 0 if q == 0 else at
        return step, q, pl.ds(at, end - at)

    def pack(tile, step, t, head):
        a11 = tile[:half_tile, :half_tile]
        a22 = tile[half_tile:, half_tile:]
        at = pl.multiple_of(HEAD + t * size, HEAD)
        send[step, pl.ds(at, half_tile), :] = jnp.where(ri <= ci, a11, a22).astype(jnp.bfloat16)
        send[step, pl.ds(at + half_tile, half_tile), :] = tile[:half_tile, half_tile:].astype(jnp.bfloat16)
        corner = jnp.sum(jnp.where(ri == ci, a22, 0.0), axis=0, keepdims=True)
        return head + jnp.where(head_row == t, corner, 0.0)

    def own_copy(k):
        step, q, span = piece(k)
        return pltpu.make_async_remote_copy(
            src_ref=send.at[step, span],
            dst_ref=recv.at[step, mine, span],
            send_sem=send_sem.at[step, q],
            recv_sem=recv_sem.at[step, mine, q],
            device_id={"col": mirror},
            device_id_type=MESH,
        )

    def pass_copy(k, j):
        step, q, span = piece(k)
        return pltpu.make_async_remote_copy(
            src_ref=recv.at[step, theirs, span],
            dst_ref=recv.at[step, theirs, span],
            send_sem=pass_sem.at[step, j, q],
            recv_sem=recv_sem.at[step, theirs, q],
            device_id={"col": first + lax.rem(mine + j, h)},
            device_id_type=MESH,
        )

    def landing(k, j):
        step, q, span = piece(k)
        sibling = lax.rem(mine + h - j, h)
        source = h - 1 - sibling
        return pltpu.make_async_remote_copy(
            src_ref=recv.at[step, source, span],
            dst_ref=recv.at[step, source, span],
            send_sem=pass_sem.at[step, j, q],
            recv_sem=recv_sem.at[step, source, q],
            device_id={"col": mirror},
            device_id_type=MESH,
        )

    pieces = 4 * rows
    begun = [0]
    direct = [0]
    sent = [0]

    def pump(upto):
        while begun[0] < min(upto, pieces):
            own_copy(begun[0]).start()
            begun[0] += 1

    def relay(upto):
        while direct[0] < min(upto, pieces):
            k = direct[0]
            if begun[0] < pieces:
                own_copy(k).wait_send()
                sent[0] += 1
                pump(k + 1 + WINDOW)
            landing(k, 0).wait_recv()
            for j in range(1, h):
                pass_copy(k, j).start()
            direct[0] += 1

    def arrive(k):
        relay(k + 1 + AHEAD)
        for j in range(1, h):
            landing(k, j).wait_recv()

    def unpack(step, t):
        for r in range(h):
            at = HEAD + t * size
            mixed = recv[step, r, pl.ds(at, half_tile), :].astype(jnp.float32)
            cross = recv[step, r, pl.ds(at + half_tile, half_tile), :]
            head = recv[step, r, 0:HEAD, :].astype(jnp.float32)
            corner = jnp.sum(jnp.where(head_row == t, head, 0.0), axis=0, keepdims=True)
            turned = mixed.T
            a11 = jnp.where(ri <= ci, mixed, turned)
            a22 = jnp.where(ri > ci, mixed, jnp.where(ri == ci, corner, turned))
            g = r * rows + t
            gath[step, g, 0:half_tile, 0:half_tile] = a11.astype(jnp.bfloat16)
            gath[step, g, half_tile:, half_tile:] = a22.astype(jnp.bfloat16)
            gath[step, g, 0:half_tile, half_tile:] = cross
            gath[step, g, half_tile:, 0:half_tile] = cross.astype(jnp.float32).T.astype(jnp.bfloat16)

    def ready(t):
        return [
            s for s in range(slots - 1)
            if max(s % rows, (s + 1) % rows) == t
        ]

    def other(step, i, s):
        first = lax.rem(cols_ref[i, s + 1], half_rows) == s
        return lax.select(first, gath[step, s], gath[step, s + 1])

    load_diag.wait()
    head = jnp.zeros((HEAD, half_tile), jnp.float32)
    for t in range(rows):
        head = pack(x[t, 0].astype(jnp.float32), 0, t, head)
    send[0, 0:HEAD, :] = head.astype(jnp.bfloat16)
    pl.semaphore_wait(barrier, n - 1)
    pump(min(WINDOW, 2 * rows))
    load_rest.wait()

    def first_diagonal(i, head):
        total = mm(x[i, 0], x[i, 0], NT)
        for s in range(1, slots):
            total += mm(x[i, s], x[i, s], NT)
        new = x[i, 0].astype(jnp.float32) + signs[0] * (total - jnp.where(eye, 0.25, 0.0))
        out_ref[i, 0] = new
        d1[i, 0] = new.astype(jnp.bfloat16)
        return pack(new, 1, i, head)

    def first_local(i, carry):
        for s in range(1, slots):
            out_ref[i, s] = x[i, s].astype(jnp.float32) + signs[0] * mm(x[i, 0], x[i, s])
        return carry

    for t in range(rows):
        if t == 0:
            head = lax.fori_loop(0, rows, first_diagonal, jnp.zeros((HEAD, half_tile), jnp.float32))
            send[1, 0:HEAD, :] = head.astype(jnp.bfloat16)
        arrive(2 * t)
        arrive(2 * t + 1)
        if t == 0:
            lax.fori_loop(0, rows, first_local, 0, unroll=True)
        unpack(0, t)
        todo = ready(t)

        def first_partner(i, carry):
            for s in todo:
                new = out_ref[i, s + 1] + signs[0] * mm(x[i, s + 1], other(0, i, s))
                low = new.astype(jnp.bfloat16)
                d1[i, s + 1] = low
                out_ref[i, s + 1] = new + signs[1] * mm(d1[i, 0], low)
            return carry

        if todo:
            lax.fori_loop(0, rows, first_partner, 0, unroll=True)

    arrive(2 * rows)
    arrive(2 * rows + 1)
    unpack(1, 0)

    def second_diagonal(i, carry):
        total = mm(d1[i, 0], d1[i, 0], NT)
        for s in range(1, slots):
            total += mm(d1[i, s], d1[i, s], NT)
        new = out_ref[i, 0] + signs[1] * (total - jnp.where(eye, 0.25, 0.0))
        out_ref[i, 0] = new
        on_diag = jnp.where(eye, new, 0.0)
        return carry + jnp.sum(jnp.sum(on_diag.reshape(size // 8, 8, 2, half_tile), axis=0), axis=1)

    lanes = lax.fori_loop(0, rows, second_diagonal, jnp.zeros((8, half_tile), jnp.float32))
    trace[me] = lanes

    def trace_copy(k):
        return pltpu.make_async_remote_copy(
            src_ref=trace.at[me],
            dst_ref=trace.at[me],
            send_sem=tsend_sem.at[k],
            recv_sem=trecv_sem.at[k],
            device_id={"col": lax.rem(me + k, n)},
            device_id_type=MESH,
        )

    def trace_landing(k):
        source = lax.rem(me + n - k, n)
        return pltpu.make_async_remote_copy(
            src_ref=trace.at[source],
            dst_ref=trace.at[source],
            send_sem=tsend_sem.at[k],
            recv_sem=trecv_sem.at[k],
            device_id={"col": lax.rem(me + k, n)},
            device_id_type=MESH,
        )

    for k in range(1, n):
        trace_copy(k).start()

    for t in range(rows):
        if t > 0:
            arrive(2 * (rows + t))
            arrive(2 * (rows + t) + 1)
            unpack(1, t)
        todo = ready(t)

        def second_partner(i, carry):
            for s in todo:
                out_ref[i, s + 1] = out_ref[i, s + 1] + signs[1] * mm(d1[i, s + 1], other(1, i, s))
            return carry

        if todo:
            lax.fori_loop(0, rows, second_partner, 0, unroll=True)

    for k in range(1, n):
        trace_landing(k).wait_recv()
        trace_copy(k).wait_send()
    total = trace[0]
    for k in range(1, n):
        total = total + trace[k]
    scale = 1.0 / (rows * n * size)
    occ_ref[...] = jnp.broadcast_to(jnp.sum(total, keepdims=True) * scale + 0.5, occ_ref.shape)

    for k in range(sent[0], pieces):
        own_copy(k).wait_send()

    for k in range(pieces):
        for j in range(1, h):
            pass_copy(k, j).wait_send()


def write_kernel(held, occ_ref, out_hbm, occ_out, sem):
    rows, slots = held.shape[0], held.shape[1]

    def part(i, j):
        span = pl.ds(2 * j, 2)
        return pltpu.make_async_copy(held.at[i, span], out_hbm.at[i, span], sem.at[i, j])

    for i in range(rows):
        for j in range(slots // 2):
            part(i, j).start()
    occ_out[...] = occ_ref[0, 0:1]
    for i in range(rows):
        for j in range(slots // 2):
            part(i, j).wait()


def shards(n, x_tiles, columns, branch):
    rows, slots, size = x_tiles.shape[0], x_tiles.shape[1], x_tiles.shape[2]
    h = n // 2
    length = HEAD + rows * size
    vmem = pl.BlockSpec(memory_space=pltpu.VMEM)
    hbm = pl.BlockSpec(memory_space=pltpu.HBM)
    flops = 2 * size**3 * rows * (slots * 2 + (slots - 1) * 4)
    held, occ = pl.pallas_call(
        functools.partial(purify_kernel, n),
        out_shape=(
            pltpu.VMEM(x_tiles.shape, jnp.float32),
            pltpu.VMEM((8, 128), jnp.float32),
        ),
        in_specs=[hbm, hbm, hbm],
        out_specs=(vmem, vmem),
        scratch_shapes=[
            pltpu.SMEM(columns.shape, jnp.int32),
            pltpu.SMEM(branch.shape, jnp.int32),
            pltpu.VMEM((rows, slots, size, size), jnp.bfloat16),
            pltpu.VMEM((rows, slots, size, size), jnp.bfloat16),
            pltpu.VMEM((2, length, size // 2), jnp.bfloat16),
            pltpu.VMEM((2, h, length, size // 2), jnp.bfloat16),
            pltpu.VMEM((2, h * rows, size, size), jnp.bfloat16),
            pltpu.VMEM((n, 8, size // 2), jnp.float32),
            pltpu.SemaphoreType.DMA((4,)),
            pltpu.SemaphoreType.DMA((2, 2 * rows)),
            pltpu.SemaphoreType.DMA((2, h, 2 * rows)),
            pltpu.SemaphoreType.DMA((2, h, 2 * rows)),
            pltpu.SemaphoreType.DMA((n,)),
            pltpu.SemaphoreType.DMA((n,)),
        ],
        compiler_params=pltpu.CompilerParams(
            collective_id=0, has_side_effects=True, vmem_limit_bytes=40 * 2**20
        ),
        cost_estimate=pl.CostEstimate(flops=flops, bytes_accessed=3 * x_tiles.size * 2, transcendentals=0),
        name="purify",
    )(*[pltpu.with_memory_space_constraint(a, pltpu.HBM) for a in (columns, branch, x_tiles)])
    return pl.pallas_call(
        write_kernel,
        out_shape=(
            jax.ShapeDtypeStruct(x_tiles.shape, jnp.float32),
            jax.ShapeDtypeStruct((1,), jnp.float32),
        ),
        in_specs=[vmem, vmem],
        out_specs=(hbm, vmem),
        scratch_shapes=[pltpu.SemaphoreType.DMA((rows, slots // 2))],
        compiler_params=pltpu.CompilerParams(vmem_limit_bytes=4 * 2**20),
        cost_estimate=pl.CostEstimate(flops=0, bytes_accessed=x_tiles.size * 4, transcendentals=0),
        name="write",
    )(
        pltpu.with_memory_space_constraint(held, pltpu.VMEM),
        pltpu.with_memory_space_constraint(occ, pltpu.VMEM),
    )


def solution(mesh):
    placed = (P(("row", "col"), None, None, None), P(("row", "col"), None), P("row", None))
    return jax.shard_map(
        functools.partial(shards, mesh.shape["col"]),
        mesh=mesh,
        in_specs=placed,
        out_specs=(P(("row", "col"), None, None, None), P("row")),
        check_vma=False,
    )
```

```python
import functools

import jax
import jax.numpy as jnp
from jax import lax
from jax.experimental import pallas as pl
from jax.experimental.pallas import tpu as pltpu
from jax.sharding import PartitionSpec as P

MESH = pl.DeviceIdType.MESH
HEAD = 16
WINDOW = 8
AHEAD = 2
NN = (((1,), (0,)), ((), ()))
NT = (((1,), (1,)), ((), ()))


def mm(a, b, dims=NN):
    return lax.dot_general(a, b, dims, preferred_element_type=jnp.float32)


def purify_kernel(
    n, cols_hbm, branch_hbm, x_hbm, out_ref, occ_ref,
    cols_ref, branch_ref, x, d1, send, recv, gath, trace, load_sem, send_sem, recv_sem, pass_sem, tsend_sem, trecv_sem,
):
    rows, slots, size = x.shape[0], x.shape[1], x.shape[2]
    half_tile = size // 2
    h = n // 2
    half_rows = rows * h
    me = lax.axis_index("col")
    upper = (me >= h).astype(jnp.int32)
    mine = me - upper * h
    first = upper * h
    mirror = n - 1 - me
    theirs = h - 1 - mine

    load_diag = pltpu.make_async_copy(x_hbm.at[:, 0:1], x.at[:, 0:1], load_sem.at[0])
    load_rest = pltpu.make_async_copy(x_hbm.at[:, 1:slots], x.at[:, 1:slots], load_sem.at[1])
    load_diag.start()
    load_cols = pltpu.make_async_copy(cols_hbm, cols_ref, load_sem.at[2])
    load_branch = pltpu.make_async_copy(branch_hbm, branch_ref, load_sem.at[3])
    load_cols.start()
    load_branch.start()
    load_rest.start()

    barrier = pltpu.get_barrier_semaphore()
    for k in range(1, n):
        pl.semaphore_signal(barrier, inc=1, device_id={"col": lax.rem(me + k, n)}, device_id_type=MESH)

    load_cols.wait()
    load_branch.wait()
    signs = [(2 * branch_ref[0, step] - 1).astype(jnp.float32) for step in range(2)]
    ri = lax.broadcasted_iota(jnp.int32, (half_tile, half_tile), 0)
    ci = lax.broadcasted_iota(jnp.int32, (half_tile, half_tile), 1)
    head_row = lax.broadcasted_iota(jnp.int32, (HEAD, half_tile), 0)
    eye = (
        lax.broadcasted_iota(jnp.int32, (size, size), 0) == lax.broadcasted_iota(jnp.int32, (size, size), 1)
    )

    def piece(k):
        step, q = divmod(k, 2 * rows)
        at, end = HEAD + q * half_tile, HEAD + (q + 1) * half_tile
        at = 0 if q == 0 else at
        return step, q, pl.ds(at, end - at)

    def pack(tile, step, t, head):
        a11 = tile[:half_tile, :half_tile]
        a22 = tile[half_tile:, half_tile:]
        at = pl.multiple_of(HEAD + t * size, HEAD)
        send[step, pl.ds(at, half_tile), :] = jnp.where(ri <= ci, a11, a22).astype(jnp.bfloat16)
        send[step, pl.ds(at + half_tile, half_tile), :] = tile[:half_tile, half_tile:].astype(jnp.bfloat16)
        corner = jnp.sum(jnp.where(ri == ci, a22, 0.0), axis=0, keepdims=True)
        return head + jnp.where(head_row == t, corner, 0.0)

    def own_copy(k):
        step, q, span = piece(k)
        return pltpu.make_async_remote_copy(
            src_ref=send.at[step, span],
            dst_ref=recv.at[step, mine, span],
            send_sem=send_sem.at[step, q],
            recv_sem=recv_sem.at[step, mine, q],
            device_id={"col": mirror},
            device_id_type=MESH,
        )

    def pass_copy(k, j):
        step, q, span = piece(k)
        return pltpu.make_async_remote_copy(
            src_ref=recv.at[step, theirs, span],
            dst_ref=recv.at[step, theirs, span],
            send_sem=pass_sem.at[step, j, q],
            recv_sem=recv_sem.at[step, theirs, q],
            device_id={"col": first + lax.rem(mine + j, h)},
            device_id_type=MESH,
        )

    def landing(k, j):
        step, q, span = piece(k)
        sibling = lax.rem(mine + h - j, h)
        source = h - 1 - sibling
        return pltpu.make_async_remote_copy(
            src_ref=recv.at[step, source, span],
            dst_ref=recv.at[step, source, span],
            send_sem=pass_sem.at[step, j, q],
            recv_sem=recv_sem.at[step, source, q],
            device_id={"col": mirror},
            device_id_type=MESH,
        )

    pieces = 4 * rows
    begun = [0]
    direct = [0]
    sent = [0]

    limit = [2 * rows]

    def pump(upto):
        while begun[0] < min(upto, limit[0]):
            if begun[0] >= WINDOW:
                own_copy(sent[0]).wait_send()
                sent[0] += 1
            own_copy(begun[0]).start()
            begun[0] += 1

    def relay(upto):
        while direct[0] < min(upto, pieces):
            k = direct[0]
            pump(k + 1 + WINDOW)
            landing(k, 0).wait_recv()
            for j in range(1, h):
                pass_copy(k, j).start()
            direct[0] += 1

    def arrive(k):
        relay(k + 1 + AHEAD)
        for j in range(1, h):
            landing(k, j).wait_recv()

    def unpack(step, t):
        for r in range(h):
            at = HEAD + t * size
            mixed = recv[step, r, pl.ds(at, half_tile), :].astype(jnp.float32)
            cross = recv[step, r, pl.ds(at + half_tile, half_tile), :]
            head = recv[step, r, 0:HEAD, :].astype(jnp.float32)
            corner = jnp.sum(jnp.where(head_row == t, head, 0.0), axis=0, keepdims=True)
            turned = mixed.T
            a11 = jnp.where(ri <= ci, mixed, turned)
            a22 = jnp.where(ri > ci, mixed, jnp.where(ri == ci, corner, turned))
            g = r * rows + t
            gath[step, g, 0:half_tile, 0:half_tile] = a11.astype(jnp.bfloat16)
            gath[step, g, half_tile:, half_tile:] = a22.astype(jnp.bfloat16)
            gath[step, g, 0:half_tile, half_tile:] = cross
            gath[step, g, half_tile:, 0:half_tile] = cross.astype(jnp.float32).T.astype(jnp.bfloat16)

    def ready(t):
        return [
            s for s in range(slots - 1)
            if max(s % rows, (s + 1) % rows) == t
        ]

    def other(step, i, s):
        first = lax.rem(cols_ref[i, s + 1], half_rows) == s
        return lax.select(first, gath[step, s], gath[step, s + 1])

    load_diag.wait()
    head = jnp.zeros((HEAD, half_tile), jnp.float32)
    for t in range(rows):
        head = pack(x[t, 0].astype(jnp.float32), 0, t, head)
    send[0, 0:HEAD, :] = head.astype(jnp.bfloat16)
    pl.semaphore_wait(barrier, n - 1)
    pump(WINDOW)
    load_rest.wait()
    relay(1)

    def first_diagonal(i, head):
        total = mm(x[i, 0], x[i, 0], NT)
        for s in range(1, slots):
            total += mm(x[i, s], x[i, s], NT)
        new = x[i, 0].astype(jnp.float32) + signs[0] * (total - jnp.where(eye, 0.25, 0.0))
        out_ref[i, 0] = new
        d1[i, 0] = new.astype(jnp.bfloat16)
        return pack(new, 1, i, head)

    def first_local(i, carry):
        for s in range(1, slots):
            out_ref[i, s] = x[i, s].astype(jnp.float32) + signs[0] * mm(x[i, 0], x[i, s])
        return carry

    for t in range(rows):
        if t == 0:
            head = lax.fori_loop(0, rows, first_diagonal, jnp.zeros((HEAD, half_tile), jnp.float32))
            send[1, 0:HEAD, :] = head.astype(jnp.bfloat16)
            limit[0] = pieces
            relay(2)
            lax.fori_loop(0, rows, first_local, 0, unroll=True)
        arrive(2 * t)
        arrive(2 * t + 1)
        unpack(0, t)
        todo = ready(t)

        def first_partner(i, carry):
            for s in todo:
                new = out_ref[i, s + 1] + signs[0] * mm(x[i, s + 1], other(0, i, s))
                low = new.astype(jnp.bfloat16)
                d1[i, s + 1] = low
                out_ref[i, s + 1] = new + signs[1] * mm(d1[i, 0], low)
            return carry

        if todo:
            lax.fori_loop(0, rows, first_partner, 0, unroll=True)

    arrive(2 * rows)
    arrive(2 * rows + 1)
    unpack(1, 0)

    def second_diagonal(i, carry):
        total = mm(d1[i, 0], d1[i, 0], NT)
        for s in range(1, slots):
            total += mm(d1[i, s], d1[i, s], NT)
        new = out_ref[i, 0] + signs[1] * (total - jnp.where(eye, 0.25, 0.0))
        out_ref[i, 0] = new
        on_diag = jnp.where(eye, new, 0.0)
        return carry + jnp.sum(jnp.sum(on_diag.reshape(size // 8, 8, 2, half_tile), axis=0), axis=1)

    lanes = lax.fori_loop(0, rows, second_diagonal, jnp.zeros((8, half_tile), jnp.float32))
    trace[me] = lanes

    def trace_copy(k):
        return pltpu.make_async_remote_copy(
            src_ref=trace.at[me],
            dst_ref=trace.at[me],
            send_sem=tsend_sem.at[k],
            recv_sem=trecv_sem.at[k],
            device_id={"col": lax.rem(me + k, n)},
            device_id_type=MESH,
        )

    def trace_landing(k):
        source = lax.rem(me + n - k, n)
        return pltpu.make_async_remote_copy(
            src_ref=trace.at[source],
            dst_ref=trace.at[source],
            send_sem=tsend_sem.at[k],
            recv_sem=trecv_sem.at[k],
            device_id={"col": lax.rem(me + k, n)},
            device_id_type=MESH,
        )

    for k in range(1, n):
        trace_copy(k).start()

    for t in range(rows):
        if t > 0:
            arrive(2 * (rows + t))
            arrive(2 * (rows + t) + 1)
            unpack(1, t)
        todo = ready(t)

        def second_partner(i, carry):
            for s in todo:
                out_ref[i, s + 1] = out_ref[i, s + 1] + signs[1] * mm(d1[i, s + 1], other(1, i, s))
            return carry

        if todo:
            lax.fori_loop(0, rows, second_partner, 0, unroll=True)

    for k in range(1, n):
        trace_landing(k).wait_recv()
        trace_copy(k).wait_send()
    total = trace[0]
    for k in range(1, n):
        total = total + trace[k]
    scale = 1.0 / (rows * n * size)
    occ_ref[...] = jnp.broadcast_to(jnp.sum(total, keepdims=True) * scale + 0.5, occ_ref.shape)

    for k in range(sent[0], pieces):
        own_copy(k).wait_send()

    for k in range(pieces):
        for j in range(1, h):
            pass_copy(k, j).wait_send()


def write_kernel(held, occ_ref, out_hbm, occ_out, sem):
    rows, slots = held.shape[0], held.shape[1]

    def part(i, j):
        span = pl.ds(2 * j, 2)
        return pltpu.make_async_copy(held.at[i, span], out_hbm.at[i, span], sem.at[i, j])

    for i in range(rows):
        for j in range(slots // 2):
            part(i, j).start()
    occ_out[...] = occ_ref[0, 0:1]
    for i in range(rows):
        for j in range(slots // 2):
            part(i, j).wait()


def shards(n, x_tiles, columns, branch):
    rows, slots, size = x_tiles.shape[0], x_tiles.shape[1], x_tiles.shape[2]
    h = n // 2
    length = HEAD + rows * size
    vmem = pl.BlockSpec(memory_space=pltpu.VMEM)
    hbm = pl.BlockSpec(memory_space=pltpu.HBM)
    flops = 2 * size**3 * rows * (slots * 2 + (slots - 1) * 4)
    held, occ = pl.pallas_call(
        functools.partial(purify_kernel, n),
        out_shape=(
            pltpu.VMEM(x_tiles.shape, jnp.float32),
            pltpu.VMEM((8, 128), jnp.float32),
        ),
        in_specs=[hbm, hbm, hbm],
        out_specs=(vmem, vmem),
        scratch_shapes=[
            pltpu.SMEM(columns.shape, jnp.int32),
            pltpu.SMEM(branch.shape, jnp.int32),
            pltpu.VMEM((rows, slots, size, size), jnp.bfloat16),
            pltpu.VMEM((rows, slots, size, size), jnp.bfloat16),
            pltpu.VMEM((2, length, size // 2), jnp.bfloat16),
            pltpu.VMEM((2, h, length, size // 2), jnp.bfloat16),
            pltpu.VMEM((2, h * rows, size, size), jnp.bfloat16),
            pltpu.VMEM((n, 8, size // 2), jnp.float32),
            pltpu.SemaphoreType.DMA((4,)),
            pltpu.SemaphoreType.DMA((2, 2 * rows)),
            pltpu.SemaphoreType.DMA((2, h, 2 * rows)),
            pltpu.SemaphoreType.DMA((2, h, 2 * rows)),
            pltpu.SemaphoreType.DMA((n,)),
            pltpu.SemaphoreType.DMA((n,)),
        ],
        compiler_params=pltpu.CompilerParams(
            collective_id=0, has_side_effects=True, vmem_limit_bytes=40 * 2**20
        ),
        cost_estimate=pl.CostEstimate(flops=flops, bytes_accessed=3 * x_tiles.size * 2, transcendentals=0),
        name="purify",
    )(*[pltpu.with_memory_space_constraint(a, pltpu.HBM) for a in (columns, branch, x_tiles)])
    return pl.pallas_call(
        write_kernel,
        out_shape=(
            jax.ShapeDtypeStruct(x_tiles.shape, jnp.float32),
            jax.ShapeDtypeStruct((1,), jnp.float32),
        ),
        in_specs=[vmem, vmem],
        out_specs=(hbm, vmem),
        scratch_shapes=[pltpu.SemaphoreType.DMA((rows, slots // 2))],
        compiler_params=pltpu.CompilerParams(vmem_limit_bytes=4 * 2**20),
        cost_estimate=pl.CostEstimate(flops=0, bytes_accessed=x_tiles.size * 4, transcendentals=0),
        name="write",
    )(
        pltpu.with_memory_space_constraint(held, pltpu.VMEM),
        pltpu.with_memory_space_constraint(occ, pltpu.VMEM),
    )


def solution(mesh):
    placed = (P(("row", "col"), None, None, None), P(("row", "col"), None), P("row", None))
    return jax.shard_map(
        functools.partial(shards, mesh.shape["col"]),
        mesh=mesh,
        in_specs=placed,
        out_specs=(P(("row", "col"), None, None, None), P("row")),
        check_vma=False,
    )
```

```python
import functools

import jax
import jax.numpy as jnp
from jax import lax
from jax.experimental import pallas as pl
from jax.experimental.pallas import tpu as pltpu
from jax.sharding import PartitionSpec as P

MESH = pl.DeviceIdType.MESH
HEAD = 16
WINDOW = 3
AHEAD = 2
NN = (((1,), (0,)), ((), ()))
NT = (((1,), (1,)), ((), ()))


def mm(a, b, dims=NN):
    return lax.dot_general(a, b, dims, preferred_element_type=jnp.float32)


def ready(rows, slots, t):
    return [s for s in range(slots - 1) if max(s % rows, (s + 1) % rows) == t]


def chosen(cols_ref, gath, i, s, half_rows):
    return lax.select(lax.rem(cols_ref[i, s + 1], half_rows) == s, gath[s], gath[s + 1])


def purify_kernel(
    n, cols_hbm, branch_hbm, x_hbm, out_ref, occ_ref, d1, gath_last,
    cols_ref, branch_ref, x, send, recv, gath_first, trace, load_sem, send_sem, recv_sem, pass_sem, tsend_sem, trecv_sem,
):
    rows, slots, size = x.shape[0], x.shape[1], x.shape[2]
    half_tile = size // 2
    h = n // 2
    half_rows = rows * h
    gath = (gath_first, gath_last)
    me = lax.axis_index("col")
    upper = (me >= h).astype(jnp.int32)
    mine = me - upper * h
    first = upper * h
    mirror = n - 1 - me
    theirs = h - 1 - mine

    load_diag = pltpu.make_async_copy(x_hbm.at[:, 0:1], x.at[:, 0:1], load_sem.at[0])
    load_rest = pltpu.make_async_copy(x_hbm.at[:, 1:slots], x.at[:, 1:slots], load_sem.at[1])
    load_diag.start()
    load_cols = pltpu.make_async_copy(cols_hbm, cols_ref, load_sem.at[2])
    load_branch = pltpu.make_async_copy(branch_hbm, branch_ref, load_sem.at[3])
    load_cols.start()
    load_branch.start()
    load_rest.start()

    barrier = pltpu.get_barrier_semaphore()
    for k in range(1, n):
        pl.semaphore_signal(barrier, inc=1, device_id={"col": lax.rem(me + k, n)}, device_id_type=MESH)

    load_cols.wait()
    load_branch.wait()
    signs = [(2 * branch_ref[0, step] - 1).astype(jnp.float32) for step in range(2)]
    ri = lax.broadcasted_iota(jnp.int32, (half_tile, half_tile), 0)
    ci = lax.broadcasted_iota(jnp.int32, (half_tile, half_tile), 1)
    head_row = lax.broadcasted_iota(jnp.int32, (HEAD, half_tile), 0)
    eye = (
        lax.broadcasted_iota(jnp.int32, (size, size), 0) == lax.broadcasted_iota(jnp.int32, (size, size), 1)
    )

    def piece(k):
        step, q = divmod(k, 2 * rows)
        at, end = HEAD + q * half_tile, HEAD + (q + 1) * half_tile
        at = 0 if q == 0 else at
        return step, q, pl.ds(at, end - at)

    def pack(tile, step, t, head):
        a11 = tile[:half_tile, :half_tile]
        a22 = tile[half_tile:, half_tile:]
        at = pl.multiple_of(HEAD + t * size, HEAD)
        send[step, pl.ds(at, half_tile), :] = jnp.where(ri <= ci, a11, a22).astype(jnp.bfloat16)
        send[step, pl.ds(at + half_tile, half_tile), :] = tile[:half_tile, half_tile:].astype(jnp.bfloat16)
        corner = jnp.sum(jnp.where(ri == ci, a22, 0.0), axis=0, keepdims=True)
        return head + jnp.where(head_row == t, corner, 0.0)

    def own_copy(k):
        step, q, span = piece(k)
        return pltpu.make_async_remote_copy(
            src_ref=send.at[step, span],
            dst_ref=recv.at[step, mine, span],
            send_sem=send_sem.at[step, q],
            recv_sem=recv_sem.at[step, mine, q],
            device_id={"col": mirror},
            device_id_type=MESH,
        )

    def pass_copy(k, j):
        step, q, span = piece(k)
        return pltpu.make_async_remote_copy(
            src_ref=recv.at[step, theirs, span],
            dst_ref=recv.at[step, theirs, span],
            send_sem=pass_sem.at[step, j, q],
            recv_sem=recv_sem.at[step, theirs, q],
            device_id={"col": first + lax.rem(mine + j, h)},
            device_id_type=MESH,
        )

    def landing(k, j):
        step, q, span = piece(k)
        sibling = lax.rem(mine + h - j, h)
        source = h - 1 - sibling
        return pltpu.make_async_remote_copy(
            src_ref=recv.at[step, source, span],
            dst_ref=recv.at[step, source, span],
            send_sem=pass_sem.at[step, j, q],
            recv_sem=recv_sem.at[step, source, q],
            device_id={"col": mirror},
            device_id_type=MESH,
        )

    pieces = 4 * rows
    begun = [0]
    direct = [0]
    sent = [0]

    limit = [2 * rows]

    def pump(upto):
        while begun[0] < min(upto, limit[0]):
            if begun[0] >= WINDOW:
                own_copy(sent[0]).wait_send()
                sent[0] += 1
            own_copy(begun[0]).start()
            begun[0] += 1

    def relay(upto):
        while direct[0] < min(upto, pieces):
            k = direct[0]
            pump(k + 1 + WINDOW)
            landing(k, 0).wait_recv()
            for j in range(1, h):
                pass_copy(k, j).start()
            direct[0] += 1

    def arrive(k):
        relay(k + 1 + AHEAD)
        for j in range(1, h):
            landing(k, j).wait_recv()

    def unpack(step, t):
        for r in range(h):
            at = HEAD + t * size
            mixed = recv[step, r, pl.ds(at, half_tile), :].astype(jnp.float32)
            cross = recv[step, r, pl.ds(at + half_tile, half_tile), :]
            head = recv[step, r, 0:HEAD, :].astype(jnp.float32)
            corner = jnp.sum(jnp.where(head_row == t, head, 0.0), axis=0, keepdims=True)
            turned = mixed.T
            a11 = jnp.where(ri <= ci, mixed, turned)
            a22 = jnp.where(ri > ci, mixed, jnp.where(ri == ci, corner, turned))
            g = r * rows + t
            gath[step][g, 0:half_tile, 0:half_tile] = a11.astype(jnp.bfloat16)
            gath[step][g, half_tile:, half_tile:] = a22.astype(jnp.bfloat16)
            gath[step][g, 0:half_tile, half_tile:] = cross
            gath[step][g, half_tile:, 0:half_tile] = cross.astype(jnp.float32).T.astype(jnp.bfloat16)

    def other(step, i, s):
        return chosen(cols_ref, gath[step], i, s, half_rows)

    load_diag.wait()
    head = jnp.zeros((HEAD, half_tile), jnp.float32)
    for t in range(rows):
        head = pack(x[t, 0].astype(jnp.float32), 0, t, head)
    send[0, 0:HEAD, :] = head.astype(jnp.bfloat16)
    pl.semaphore_wait(barrier, n - 1)
    pump(WINDOW)
    load_rest.wait()

    def first_diagonal(i, head):
        total = mm(x[i, 0], x[i, 0], NT)
        for s in range(1, slots):
            total += mm(x[i, s], x[i, s], NT)
        new = x[i, 0].astype(jnp.float32) + signs[0] * (total - jnp.where(eye, 0.25, 0.0))
        out_ref[i, 0] = new
        d1[i, 0] = new.astype(jnp.bfloat16)
        return pack(new, 1, i, head)

    def first_local(i, carry):
        for s in range(1, slots):
            out_ref[i, s] = x[i, s].astype(jnp.float32) + signs[0] * mm(x[i, 0], x[i, s])
        return carry

    for t in range(rows):
        if t == 0:
            head = lax.fori_loop(0, rows, first_diagonal, jnp.zeros((HEAD, half_tile), jnp.float32))
            send[1, 0:HEAD, :] = head.astype(jnp.bfloat16)
            limit[0] = pieces
            relay(2)
            lax.fori_loop(0, rows, first_local, 0, unroll=True)
        arrive(2 * t)
        arrive(2 * t + 1)
        unpack(0, t)
        todo = ready(rows, slots, t)

        def first_partner(i, carry):
            for s in todo:
                new = out_ref[i, s + 1] + signs[0] * mm(x[i, s + 1], other(0, i, s))
                low = new.astype(jnp.bfloat16)
                d1[i, s + 1] = low
                out_ref[i, s + 1] = new + signs[1] * mm(d1[i, 0], low)
            return carry

        if todo:
            lax.fori_loop(0, rows, first_partner, 0, unroll=True)

    arrive(2 * rows)
    arrive(2 * rows + 1)
    unpack(1, 0)

    def second_diagonal(i, carry):
        total = mm(d1[i, 0], d1[i, 0], NT)
        for s in range(1, slots):
            total += mm(d1[i, s], d1[i, s], NT)
        new = out_ref[i, 0] + signs[1] * (total - jnp.where(eye, 0.25, 0.0))
        out_ref[i, 0] = new
        on_diag = jnp.where(eye, new, 0.0)
        return carry + jnp.sum(jnp.sum(on_diag.reshape(size // 8, 8, 2, half_tile), axis=0), axis=1)

    lanes = lax.fori_loop(0, rows, second_diagonal, jnp.zeros((8, half_tile), jnp.float32))
    trace[me] = lanes

    def trace_copy(k):
        return pltpu.make_async_remote_copy(
            src_ref=trace.at[me],
            dst_ref=trace.at[me],
            send_sem=tsend_sem.at[k],
            recv_sem=trecv_sem.at[k],
            device_id={"col": lax.rem(me + k, n)},
            device_id_type=MESH,
        )

    def trace_landing(k):
        source = lax.rem(me + n - k, n)
        return pltpu.make_async_remote_copy(
            src_ref=trace.at[source],
            dst_ref=trace.at[source],
            send_sem=tsend_sem.at[k],
            recv_sem=trecv_sem.at[k],
            device_id={"col": lax.rem(me + k, n)},
            device_id_type=MESH,
        )

    for k in range(1, n):
        trace_copy(k).start()

    for t in range(rows):
        if t > 0:
            arrive(2 * (rows + t))
            arrive(2 * (rows + t) + 1)
            unpack(1, t)
        todo = ready(rows, slots, t)

        def second_partner(i, carry):
            for s in todo:
                out_ref[i, s + 1] = out_ref[i, s + 1] + signs[1] * mm(d1[i, s + 1], other(1, i, s))
            return carry

        if todo and t < rows - 1:
            lax.fori_loop(0, rows, second_partner, 0, unroll=True)

    for k in range(1, n):
        trace_landing(k).wait_recv()
        trace_copy(k).wait_send()
    total = trace[0]
    for k in range(1, n):
        total = total + trace[k]
    scale = 1.0 / (rows * n * size)
    occ_ref[...] = jnp.broadcast_to(jnp.sum(total, keepdims=True) * scale + 0.5, occ_ref.shape)

    for k in range(sent[0], pieces):
        own_copy(k).wait_send()

    for k in range(pieces):
        for j in range(1, h):
            pass_copy(k, j).wait_send()


def write_kernel(cols_hbm, branch_hbm, held, occ_ref, d1, gath, out_hbm, occ_out, cols_ref, branch_ref, fresh, load_sem, sem):
    rows, slots = held.shape[0], held.shape[1]
    half_rows = gath.shape[0]
    todo = ready(rows, slots, rows - 1)
    load_cols = pltpu.make_async_copy(cols_hbm, cols_ref, load_sem.at[0])
    load_branch = pltpu.make_async_copy(branch_hbm, branch_ref, load_sem.at[1])
    load_cols.start()
    load_branch.start()

    def part(i, j):
        source = fresh.at[i, todo.index(j - 1)] if j - 1 in todo else held.at[i, j]
        return pltpu.make_async_copy(source, out_hbm.at[i, j], sem.at[i, j])

    for i in range(rows):
        for j in range(slots):
            if j - 1 not in todo:
                part(i, j).start()
    occ_out[...] = occ_ref[0, 0:1]
    load_cols.wait()
    load_branch.wait()
    sign = (2 * branch_ref[0, 1] - 1).astype(jnp.float32)
    for i in range(rows):
        for at, s in enumerate(todo):
            partner = mm(d1[i, s + 1], chosen(cols_ref, gath, i, s, half_rows))
            fresh[i, at] = held[i, s + 1] + sign * partner
            part(i, s + 1).start()
    for i in range(rows):
        for j in range(slots):
            part(i, j).wait()


def shards(n, x_tiles, columns, branch):
    rows, slots, size = x_tiles.shape[0], x_tiles.shape[1], x_tiles.shape[2]
    h = n // 2
    last = len(ready(rows, slots, rows - 1))
    length = HEAD + rows * size
    vmem = pl.BlockSpec(memory_space=pltpu.VMEM)
    hbm = pl.BlockSpec(memory_space=pltpu.HBM)
    flops = 2 * size**3 * rows * (slots * 2 + (slots - 1) * 4)
    held, occ, low, gath = pl.pallas_call(
        functools.partial(purify_kernel, n),
        out_shape=(
            pltpu.VMEM(x_tiles.shape, jnp.float32),
            pltpu.VMEM((8, 128), jnp.float32),
            pltpu.VMEM(x_tiles.shape, jnp.bfloat16),
            pltpu.VMEM((h * rows, size, size), jnp.bfloat16),
        ),
        in_specs=[hbm, hbm, hbm],
        out_specs=(vmem, vmem, vmem, vmem),
        scratch_shapes=[
            pltpu.SMEM(columns.shape, jnp.int32),
            pltpu.SMEM(branch.shape, jnp.int32),
            pltpu.VMEM((rows, slots, size, size), jnp.bfloat16),
            pltpu.VMEM((2, length, size // 2), jnp.bfloat16),
            pltpu.VMEM((2, h, length, size // 2), jnp.bfloat16),
            pltpu.VMEM((h * rows, size, size), jnp.bfloat16),
            pltpu.VMEM((n, 8, size // 2), jnp.float32),
            pltpu.SemaphoreType.DMA((4,)),
            pltpu.SemaphoreType.DMA((2, 2 * rows)),
            pltpu.SemaphoreType.DMA((2, h, 2 * rows)),
            pltpu.SemaphoreType.DMA((2, h, 2 * rows)),
            pltpu.SemaphoreType.DMA((n,)),
            pltpu.SemaphoreType.DMA((n,)),
        ],
        compiler_params=pltpu.CompilerParams(
            collective_id=0, has_side_effects=True, vmem_limit_bytes=32 * 2**20
        ),
        cost_estimate=pl.CostEstimate(flops=flops, bytes_accessed=3 * x_tiles.size * 2, transcendentals=0),
        name="purify",
    )(*[pltpu.with_memory_space_constraint(a, pltpu.HBM) for a in (columns, branch, x_tiles)])
    return pl.pallas_call(
        write_kernel,
        out_shape=(
            jax.ShapeDtypeStruct(x_tiles.shape, jnp.float32),
            jax.ShapeDtypeStruct((1,), jnp.float32),
        ),
        in_specs=[hbm, hbm, vmem, vmem, vmem, vmem],
        out_specs=(hbm, vmem),
        scratch_shapes=[
            pltpu.SMEM(columns.shape, jnp.int32),
            pltpu.SMEM(branch.shape, jnp.int32),
            pltpu.VMEM((rows, last, size, size), jnp.float32),
            pltpu.SemaphoreType.DMA((2,)),
            pltpu.SemaphoreType.DMA((rows, slots)),
        ],
        compiler_params=pltpu.CompilerParams(vmem_limit_bytes=12 * 2**20),
        cost_estimate=pl.CostEstimate(flops=0, bytes_accessed=x_tiles.size * 4, transcendentals=0),
        name="write",
    )(
        pltpu.with_memory_space_constraint(columns, pltpu.HBM),
        pltpu.with_memory_space_constraint(branch, pltpu.HBM),
        *[pltpu.with_memory_space_constraint(a, pltpu.VMEM) for a in (held, occ, low, gath)],
    )


def solution(mesh):
    placed = (P(("row", "col"), None, None, None), P(("row", "col"), None), P("row", None))
    return jax.shard_map(
        functools.partial(shards, mesh.shape["col"]),
        mesh=mesh,
        in_specs=placed,
        out_specs=(P(("row", "col"), None, None, None), P("row")),
        check_vma=False,
    )
```

```python
import functools

import jax
import jax.numpy as jnp
from jax import lax
from jax.experimental import pallas as pl
from jax.experimental.pallas import tpu as pltpu
from jax.sharding import PartitionSpec as P

MESH = pl.DeviceIdType.MESH
HEAD = 16
WINDOW = 2
AHEAD = 2
NN = (((1,), (0,)), ((), ()))
NT = (((1,), (1,)), ((), ()))


def mm(a, b, dims=NN):
    return lax.dot_general(a, b, dims, preferred_element_type=jnp.float32)


def ready(rows, slots, t):
    return [s for s in range(slots - 1) if max(s % rows, (s + 1) % rows) == t]


def chosen(cols_ref, gath, i, s, half_rows):
    return lax.select(lax.rem(cols_ref[i, s + 1], half_rows) == s, gath[s], gath[s + 1])


def purify_kernel(
    n, cols_hbm, branch_hbm, x_hbm, out_ref, occ_ref, d1, gath_last,
    cols_ref, branch_ref, x, send, recv, gath_first, trace, load_sem, send_sem, recv_sem, pass_sem, tsend_sem, trecv_sem,
):
    rows, slots, size = x.shape[0], x.shape[1], x.shape[2]
    half_tile = size // 2
    h = n // 2
    half_rows = rows * h
    gath = (gath_first, gath_last)
    me = lax.axis_index("col")
    upper = (me >= h).astype(jnp.int32)
    mine = me - upper * h
    first = upper * h
    mirror = n - 1 - me
    theirs = h - 1 - mine

    load_diag = pltpu.make_async_copy(x_hbm.at[:, 0:1], x.at[:, 0:1], load_sem.at[0])
    load_rest = pltpu.make_async_copy(x_hbm.at[:, 1:slots], x.at[:, 1:slots], load_sem.at[1])
    load_diag.start()
    load_cols = pltpu.make_async_copy(cols_hbm, cols_ref, load_sem.at[2])
    load_branch = pltpu.make_async_copy(branch_hbm, branch_ref, load_sem.at[3])
    load_cols.start()
    load_branch.start()
    load_rest.start()

    barrier = pltpu.get_barrier_semaphore()
    for k in range(1, n):
        pl.semaphore_signal(barrier, inc=1, device_id={"col": lax.rem(me + k, n)}, device_id_type=MESH)

    load_cols.wait()
    load_branch.wait()
    signs = [(2 * branch_ref[0, step] - 1).astype(jnp.float32) for step in range(2)]
    ri = lax.broadcasted_iota(jnp.int32, (half_tile, half_tile), 0)
    ci = lax.broadcasted_iota(jnp.int32, (half_tile, half_tile), 1)
    head_row = lax.broadcasted_iota(jnp.int32, (HEAD, half_tile), 0)
    eye = (
        lax.broadcasted_iota(jnp.int32, (size, size), 0) == lax.broadcasted_iota(jnp.int32, (size, size), 1)
    )

    def piece(k):
        step, q = divmod(k, 2 * rows)
        at, end = HEAD + q * half_tile, HEAD + (q + 1) * half_tile
        at = 0 if q == 0 else at
        return step, q, pl.ds(at, end - at)

    def pack(tile, step, t, head):
        a11 = tile[:half_tile, :half_tile]
        a22 = tile[half_tile:, half_tile:]
        at = pl.multiple_of(HEAD + t * size, HEAD)
        send[step, pl.ds(at, half_tile), :] = jnp.where(ri <= ci, a11, a22).astype(jnp.bfloat16)
        send[step, pl.ds(at + half_tile, half_tile), :] = tile[:half_tile, half_tile:].astype(jnp.bfloat16)
        corner = jnp.sum(jnp.where(ri == ci, a22, 0.0), axis=0, keepdims=True)
        return head + jnp.where(head_row == t, corner, 0.0)

    def own_copy(k):
        step, q, span = piece(k)
        return pltpu.make_async_remote_copy(
            src_ref=send.at[step, span],
            dst_ref=recv.at[step, mine, span],
            send_sem=send_sem.at[step, q],
            recv_sem=recv_sem.at[step, mine, q],
            device_id={"col": mirror},
            device_id_type=MESH,
        )

    def pass_copy(k, j):
        step, q, span = piece(k)
        return pltpu.make_async_remote_copy(
            src_ref=recv.at[step, theirs, span],
            dst_ref=recv.at[step, theirs, span],
            send_sem=pass_sem.at[step, j, q],
            recv_sem=recv_sem.at[step, theirs, q],
            device_id={"col": first + lax.rem(mine + j, h)},
            device_id_type=MESH,
        )

    def landing(k, j):
        step, q, span = piece(k)
        sibling = lax.rem(mine + h - j, h)
        source = h - 1 - sibling
        return pltpu.make_async_remote_copy(
            src_ref=recv.at[step, source, span],
            dst_ref=recv.at[step, source, span],
            send_sem=pass_sem.at[step, j, q],
            recv_sem=recv_sem.at[step, source, q],
            device_id={"col": mirror},
            device_id_type=MESH,
        )

    pieces = 4 * rows
    begun = [0]
    direct = [0]
    sent = [0]

    limit = [2 * rows]

    def pump(upto):
        while begun[0] < min(upto, limit[0]):
            if begun[0] >= WINDOW:
                own_copy(sent[0]).wait_send()
                sent[0] += 1
            own_copy(begun[0]).start()
            begun[0] += 1

    def relay(upto):
        while direct[0] < min(upto, pieces):
            k = direct[0]
            pump(k + 1 + WINDOW)
            landing(k, 0).wait_recv()
            for j in range(1, h):
                pass_copy(k, j).start()
            direct[0] += 1

    def arrive(k):
        relay(k + 1 + AHEAD)
        for j in range(1, h):
            landing(k, j).wait_recv()

    def unpack(step, t):
        for r in range(h):
            at = HEAD + t * size
            mixed = recv[step, r, pl.ds(at, half_tile), :].astype(jnp.float32)
            cross = recv[step, r, pl.ds(at + half_tile, half_tile), :]
            head = recv[step, r, 0:HEAD, :].astype(jnp.float32)
            corner = jnp.sum(jnp.where(head_row == t, head, 0.0), axis=0, keepdims=True)
            turned = mixed.T
            a11 = jnp.where(ri <= ci, mixed, turned)
            a22 = jnp.where(ri > ci, mixed, jnp.where(ri == ci, corner, turned))
            g = r * rows + t
            gath[step][g, 0:half_tile, 0:half_tile] = a11.astype(jnp.bfloat16)
            gath[step][g, half_tile:, half_tile:] = a22.astype(jnp.bfloat16)
            gath[step][g, 0:half_tile, half_tile:] = cross
            gath[step][g, half_tile:, 0:half_tile] = cross.astype(jnp.float32).T.astype(jnp.bfloat16)

    def other(step, i, s):
        return chosen(cols_ref, gath[step], i, s, half_rows)

    load_diag.wait()
    head = jnp.zeros((HEAD, half_tile), jnp.float32)
    for t in range(rows):
        head = pack(x[t, 0].astype(jnp.float32), 0, t, head)
    send[0, 0:HEAD, :] = head.astype(jnp.bfloat16)
    pl.semaphore_wait(barrier, n - 1)
    pump(WINDOW)
    load_rest.wait()

    def first_diagonal(i, head):
        total = mm(x[i, 0], x[i, 0], NT)
        for s in range(1, slots):
            total += mm(x[i, s], x[i, s], NT)
        new = x[i, 0].astype(jnp.float32) + signs[0] * (total - jnp.where(eye, 0.25, 0.0))
        out_ref[i, 0] = new
        d1[i, 0] = new.astype(jnp.bfloat16)
        return pack(new, 1, i, head)

    def first_local(i, carry):
        for s in range(1, slots):
            out_ref[i, s] = x[i, s].astype(jnp.float32) + signs[0] * mm(x[i, 0], x[i, s])
        return carry

    for t in range(rows):
        if t == 0:
            head = lax.fori_loop(0, rows, first_diagonal, jnp.zeros((HEAD, half_tile), jnp.float32))
            send[1, 0:HEAD, :] = head.astype(jnp.bfloat16)
            limit[0] = pieces
            relay(2)
            lax.fori_loop(0, rows, first_local, 0, unroll=True)
        arrive(2 * t)
        arrive(2 * t + 1)
        unpack(0, t)
        todo = ready(rows, slots, t)

        def first_partner(i, carry):
            for s in todo:
                new = out_ref[i, s + 1] + signs[0] * mm(x[i, s + 1], other(0, i, s))
                low = new.astype(jnp.bfloat16)
                d1[i, s + 1] = low
                out_ref[i, s + 1] = new + signs[1] * mm(d1[i, 0], low)
            return carry

        if todo:
            lax.fori_loop(0, rows, first_partner, 0, unroll=True)

    arrive(2 * rows)
    arrive(2 * rows + 1)
    unpack(1, 0)

    def second_diagonal(i, carry):
        total = mm(d1[i, 0], d1[i, 0], NT)
        for s in range(1, slots):
            total += mm(d1[i, s], d1[i, s], NT)
        new = out_ref[i, 0] + signs[1] * (total - jnp.where(eye, 0.25, 0.0))
        out_ref[i, 0] = new
        on_diag = jnp.where(eye, new, 0.0)
        return carry + jnp.sum(jnp.sum(on_diag.reshape(size // 8, 8, 2, half_tile), axis=0), axis=1)

    lanes = jnp.zeros((8, half_tile), jnp.float32)
    middle = rows // 2
    if middle:
        lanes = lax.fori_loop(0, middle, second_diagonal, lanes)
        relay(direct[0] + 1)
    lanes = lax.fori_loop(middle, rows, second_diagonal, lanes)
    trace[me] = lanes

    def trace_copy(k):
        return pltpu.make_async_remote_copy(
            src_ref=trace.at[me],
            dst_ref=trace.at[me],
            send_sem=tsend_sem.at[k],
            recv_sem=trecv_sem.at[k],
            device_id={"col": lax.rem(me + k, n)},
            device_id_type=MESH,
        )

    def trace_landing(k):
        source = lax.rem(me + n - k, n)
        return pltpu.make_async_remote_copy(
            src_ref=trace.at[source],
            dst_ref=trace.at[source],
            send_sem=tsend_sem.at[k],
            recv_sem=trecv_sem.at[k],
            device_id={"col": lax.rem(me + k, n)},
            device_id_type=MESH,
        )

    for k in range(1, n):
        trace_copy(k).start()

    for t in range(rows):
        if t > 0:
            arrive(2 * (rows + t))
            arrive(2 * (rows + t) + 1)
            unpack(1, t)
        todo = ready(rows, slots, t)

        def second_partner(i, carry):
            for s in todo:
                out_ref[i, s + 1] = out_ref[i, s + 1] + signs[1] * mm(d1[i, s + 1], other(1, i, s))
            return carry

        if todo and t < rows - 1:
            lax.fori_loop(0, rows, second_partner, 0, unroll=True)

    for k in range(1, n):
        trace_landing(k).wait_recv()
        trace_copy(k).wait_send()
    total = trace[0]
    for k in range(1, n):
        total = total + trace[k]
    scale = 1.0 / (rows * n * size)
    occ_ref[...] = jnp.broadcast_to(jnp.sum(total, keepdims=True) * scale + 0.5, occ_ref.shape)

    for k in range(sent[0], pieces):
        own_copy(k).wait_send()

    for k in range(pieces):
        for j in range(1, h):
            pass_copy(k, j).wait_send()


def write_kernel(cols_hbm, branch_hbm, held, occ_ref, d1, gath, out_hbm, occ_out, cols_ref, branch_ref, fresh, load_sem, sem):
    rows, slots = held.shape[0], held.shape[1]
    half_rows = gath.shape[0]
    todo = ready(rows, slots, rows - 1)
    load_cols = pltpu.make_async_copy(cols_hbm, cols_ref, load_sem.at[0])
    load_branch = pltpu.make_async_copy(branch_hbm, branch_ref, load_sem.at[1])
    load_cols.start()
    load_branch.start()

    def part(i, j):
        source = fresh.at[i, todo.index(j - 1)] if j - 1 in todo else held.at[i, j]
        return pltpu.make_async_copy(source, out_hbm.at[i, j], sem.at[i, j])

    for i in range(rows):
        for j in range(slots):
            if j - 1 not in todo:
                part(i, j).start()
    occ_out[...] = occ_ref[0, 0:1]
    load_cols.wait()
    load_branch.wait()
    sign = (2 * branch_ref[0, 1] - 1).astype(jnp.float32)
    for i in range(rows):
        for at, s in enumerate(todo):
            partner = mm(d1[i, s + 1], chosen(cols_ref, gath, i, s, half_rows))
            fresh[i, at] = held[i, s + 1] + sign * partner
            part(i, s + 1).start()
    for i in range(rows):
        for j in range(slots):
            part(i, j).wait()


def shards(n, x_tiles, columns, branch):
    rows, slots, size = x_tiles.shape[0], x_tiles.shape[1], x_tiles.shape[2]
    h = n // 2
    last = len(ready(rows, slots, rows - 1))
    length = HEAD + rows * size
    vmem = pl.BlockSpec(memory_space=pltpu.VMEM)
    hbm = pl.BlockSpec(memory_space=pltpu.HBM)
    flops = 2 * size**3 * rows * (slots * 2 + (slots - 1) * 4)
    held, occ, low, gath = pl.pallas_call(
        functools.partial(purify_kernel, n),
        out_shape=(
            pltpu.VMEM(x_tiles.shape, jnp.float32),
            pltpu.VMEM((8, 128), jnp.float32),
            pltpu.VMEM(x_tiles.shape, jnp.bfloat16),
            pltpu.VMEM((h * rows, size, size), jnp.bfloat16),
        ),
        in_specs=[hbm, hbm, hbm],
        out_specs=(vmem, vmem, vmem, vmem),
        scratch_shapes=[
            pltpu.SMEM(columns.shape, jnp.int32),
            pltpu.SMEM(branch.shape, jnp.int32),
            pltpu.VMEM((rows, slots, size, size), jnp.bfloat16),
            pltpu.VMEM((2, length, size // 2), jnp.bfloat16),
            pltpu.VMEM((2, h, length, size // 2), jnp.bfloat16),
            pltpu.VMEM((h * rows, size, size), jnp.bfloat16),
            pltpu.VMEM((n, 8, size // 2), jnp.float32),
            pltpu.SemaphoreType.DMA((4,)),
            pltpu.SemaphoreType.DMA((2, 2 * rows)),
            pltpu.SemaphoreType.DMA((2, h, 2 * rows)),
            pltpu.SemaphoreType.DMA((2, h, 2 * rows)),
            pltpu.SemaphoreType.DMA((n,)),
            pltpu.SemaphoreType.DMA((n,)),
        ],
        compiler_params=pltpu.CompilerParams(
            collective_id=0, has_side_effects=True, vmem_limit_bytes=32 * 2**20
        ),
        cost_estimate=pl.CostEstimate(flops=flops, bytes_accessed=3 * x_tiles.size * 2, transcendentals=0),
        name="purify",
    )(*[pltpu.with_memory_space_constraint(a, pltpu.HBM) for a in (columns, branch, x_tiles)])
    return pl.pallas_call(
        write_kernel,
        out_shape=(
            jax.ShapeDtypeStruct(x_tiles.shape, jnp.float32),
            jax.ShapeDtypeStruct((1,), jnp.float32),
        ),
        in_specs=[hbm, hbm, vmem, vmem, vmem, vmem],
        out_specs=(hbm, vmem),
        scratch_shapes=[
            pltpu.SMEM(columns.shape, jnp.int32),
            pltpu.SMEM(branch.shape, jnp.int32),
            pltpu.VMEM((rows, last, size, size), jnp.float32),
            pltpu.SemaphoreType.DMA((2,)),
            pltpu.SemaphoreType.DMA((rows, slots)),
        ],
        compiler_params=pltpu.CompilerParams(vmem_limit_bytes=12 * 2**20),
        cost_estimate=pl.CostEstimate(flops=0, bytes_accessed=x_tiles.size * 4, transcendentals=0),
        name="write",
    )(
        pltpu.with_memory_space_constraint(columns, pltpu.HBM),
        pltpu.with_memory_space_constraint(branch, pltpu.HBM),
        *[pltpu.with_memory_space_constraint(a, pltpu.VMEM) for a in (held, occ, low, gath)],
    )


def solution(mesh):
    placed = (P(("row", "col"), None, None, None), P(("row", "col"), None), P("row", None))
    return jax.shard_map(
        functools.partial(shards, mesh.shape["col"]),
        mesh=mesh,
        in_specs=placed,
        out_specs=(P(("row", "col"), None, None, None), P("row")),
        check_vma=False,
    )
```
